1024 devices in a mesh: member: 8 (over y), lat: 32 (over z, x_hi), lon: 4 (over x_lo, core).
Axes of the slice: x: 8 (x_hi: 4, x_lo: 2; x = x_hi * 2 + x_lo), y: 8, z: 8, core: 2. Of those that a mesh axis runs over, the one named last changes fastest.
Arguments:
- members: bfloat16 [8, 16, 768, 1024], P('member', None, 'lat', 'lon'), may hold values from -9 to 9, as said below
- observed: bfloat16 [16, 768, 1024], P(None, 'lat', 'lon'), may hold values from -6 to 6
- scales: float32 [16], replicated, may hold values from 0.5 to 2
Outputs:
- cell_grad: float32 [8, 16, 768, 1024], P('member', None, 'lat', 'lon')
The draws below stay inside these ranges and needn't reach their ends.
Inputs may be any that keep to these rules, and one draw needn't show every extreme that they name: `members`: each member is a zonal pattern of its own plus a field that varies from cell to cell.
All inputs are finite; a program needn't handle non-finite values.
Results may differ from the reference program's by a relative error of at most 0.0003.
Values may be sent and summed in bfloat16 or wider, within the bound.
No kernel may reach another device: no remote copies, remote signals or barrier semaphores. Data moves between devices by JAX's collectives and lax.ppermute only.
A program may use at most 32 MiB of HBM per device.

```python
import math
import jax
import jax.numpy as jnp
from jax import lax

C = 16
M = 8
LAT = 768
LON = 1024


def draw_members(key, part):
    key = jax.random.fold_in(key, 1)
    key_zonal, key_noise = jax.random.split(key)
    pattern = 0.5 * jnp.clip(jax.random.normal(key_zonal, (M, C, LAT, 1), jnp.float32), -3.0, 3.0)
    rows = jnp.arange(LAT).astype(jnp.float32) / LAT
    row_scale = 0.6 * jnp.exp(jnp.log(3.0) * rows)
    noise = jnp.clip(jax.random.normal(key_noise, (M, C, LAT, LON), jnp.float32), -4.0, 4.0)
    return (pattern + noise * row_scale[None, None, :, None]).astype(jnp.bfloat16)


def block_levels(rng, shape, cuts, smallest, top_value):
    def one(position, parts):
        draws = jax.random.uniform(jax.random.fold_in(jax.random.fold_in(rng, 6), position), (parts,), jnp.float32, smallest / len(cuts), top_value / len(cuts))
        return jnp.repeat(jnp.exp(draws), shape[position] // parts).reshape((-1,) + (1,) * (len(shape) - position - 1))

    gain = one(*cuts[0])
    for cut in cuts[1:]:
        gain = gain * one(*cut)
    return gain


def scatter_about(own_key, dims, deviation, most, pieces=(), held_as=jnp.bfloat16):
    drawn = jax.random.normal(own_key, dims, jnp.float32) * deviation
    if len(pieces) > 0:
        drawn = block_levels(own_key, dims, pieces, -0.22, 0.18) * drawn
    return jnp.clip(drawn, min=-most, max=most).astype(held_as)


def setup_inputs(seed: int = 0) -> dict:
    key_list = jax.random.split(jax.random.key(seed), 4)
    return {
        "members": draw_members(jax.random.fold_in(key_list[3], 71), 0),
        "observed": scatter_about(key_list[1], (C, LAT, LON), 1.0, 6.0, ((1, 32), (2, 4))),
        "scales": jnp.clip(jnp.exp(jax.random.uniform(key_list[2], (C,), jnp.float32, math.log(0.5), math.log(2.0))), 0.5, 2.0),
    }


BAND = 1.0


def lat_weights(count):
    index = jnp.arange(count).astype(jnp.float32)
    angle = (-90.0 + (index + 0.5) * 180.0 / count) * (jnp.pi / 180.0)
    return jnp.cos(angle)


def reference(members, observed, scales):
    xfull = members.astype(jnp.float32)
    yfull = observed.astype(jnp.float32)
    weights = lat_weights(LAT)
    sumw = jnp.sum(weights)
    inv_sq = 1.0 / (scales * scales)
    field_wgt = weights[None, :, None] * inv_sq[:, None, None] / (C * LON * sumw)

    def field_row(xrow):
        return lax.map(lambda other: jnp.sum(field_wgt * (xrow - other) ** 2), xfull)

    dist = lax.map(field_row, xfull)
    dobs = lax.map(lambda xrow: jnp.sum(field_wgt * (xrow - yfull) ** 2), xfull)
    zonal = jnp.sum(xfull, axis=3) / LON
    zobs = jnp.sum(yfull, axis=2) / LON
    zonal_wgt = weights[None, :] * inv_sq[:, None] / (C * sumw)
    zdist = jnp.sum(zonal_wgt[None, None] * (zonal[:, None] - zonal[None, :]) ** 2, axis=(2, 3))
    zdobs = jnp.sum(zonal_wgt[None] * (zonal - zobs[None]) ** 2, axis=(1, 2))
    offdiag = 1.0 - jnp.eye(M, dtype=jnp.float32)
    acoef = jnp.exp(-dist / (2.0 * BAND)) / (M * (M - 1) * BAND) * offdiag
    bcoef = jnp.exp(-dobs / (2.0 * BAND)) / (M * BAND)
    zacoef = jnp.exp(-zdist / (2.0 * BAND)) / (M * (M - 1) * BAND) * offdiag
    zbcoef = jnp.exp(-zdobs / (2.0 * BAND)) / (M * BAND)
    mixed = jnp.einsum("mn,nclw->mclw", acoef, xfull, precision=lax.Precision.HIGHEST)
    field_term = -jnp.sum(acoef, axis=1)[:, None, None, None] * xfull + mixed + bcoef[:, None, None, None] * (xfull - yfull[None])
    zmixed = jnp.einsum("mn,ncl->mcl", zacoef, zonal, precision=lax.Precision.HIGHEST)
    zonal_term = -jnp.sum(zacoef, axis=1)[:, None, None] * zonal + zmixed + zbcoef[:, None, None] * (zonal - zobs[None])
    factor = LAT * weights[None, :, None] * inv_sq[:, None, None] / sumw
    return factor[None] * (field_term + zonal_term[..., None])
```

```python
import functools

import jax
import jax.numpy as jnp
import numpy as np
from jax import lax
from jax.experimental import pallas as pl
from jax.experimental.pallas import tpu as pltpu
from jax.sharding import Mesh
from jax.sharding import PartitionSpec as P

BAND = 1.0
F32 = jnp.float32
BF16 = jnp.bfloat16
C, M, LAT, LON = 16, 8, 768, 1024
ROWS, COLS = 24, 256
CELLS = C * ROWS
GROUP = 32
HIGHEST = lax.Precision.HIGHEST


def total_weight():
    index = np.arange(LAT).astype(np.float32)
    angle = (np.float32(-90.0) + (index + np.float32(0.5)) * np.float32(180.0) / np.float32(LAT)) * np.float32(
        np.pi / 180.0
    )
    return float(np.sum(np.cos(angle.astype(np.float32)).astype(np.float64)))


SUMW = total_weight()


def row_weight(index):
    angle = (-90.0 + (index.astype(F32) + 0.5) * 180.0 / LAT) * np.float32(np.pi / 180.0)
    return jnp.cos(angle)


def iota(shape, axis):
    return lax.broadcasted_iota(jnp.int32, shape, axis)


def lat_index():
    return lax.axis_index("z") * 4 + lax.axis_index("xh")


def tile_weights(shape):
    return row_weight(lat_index() * ROWS + iota(shape, 0))


def inverse_square(scales_ref, c):
    s = scales_ref[c]
    return 1.0 / (s * s)


def lanes_sum(x):
    ones = jnp.ones((8, COLS), BF16)
    flat = x.reshape(CELLS, COLS).astype(BF16)
    return lax.dot_general(ones, flat, (((1,), (1,)), ((), ())), preferred_element_type=F32)


def part_of(part, block, lane):
    flat = block * 128 + lane
    return (flat >= part * (CELLS // M)) & (flat < (part + 1) * (CELLS // M))


def pack_kernel(own_ref, obs_ref, pay_ref):
    me = lax.axis_index("y")
    x = own_ref[0].astype(F32)
    zx = lanes_sum(x)
    zy = lanes_sum(obs_ref[...].astype(F32))
    row, lane = iota((8, 128), 0), iota((8, 128), 1)

    def high(v):
        return v.astype(BF16).astype(F32)

    part = jnp.zeros((8, 128), F32)
    extra = jnp.zeros((8, 128), F32)
    for k in range(3):
        part = jnp.where(part_of(me, k, lane), zy[:, k * 128 : (k + 1) * 128], part)
        zk = zx[:, k * 128 : (k + 1) * 128]
        extra = jnp.where(row == k, high(zk), extra)
        extra = jnp.where(row == k + 3, zk - high(zk), extra)
    extra = jnp.where(row == 6, high(part), extra)
    extra = jnp.where(row == 7, part - high(part), extra)
    for d in range(GROUP):
        h = d % 2
        pay_ref[d] = jnp.concatenate([x[d // 2, :, h * 128 : (h + 1) * 128], extra], axis=0).astype(BF16)


def local_kernel(scales_ref, own_ref, obs_ref, aux_ref):
    w = tile_weights((ROWS, 128))
    total = jnp.zeros((ROWS, 128), F32)
    for c in range(C):
        d = own_ref[0, c].astype(F32) - obs_ref[c].astype(F32)
        d = d * d
        total = total + (d[:, :128] + d[:, 128:]) * inverse_square(scales_ref, c)
    total = total * w
    aux_ref[0:8] = (total[0:8] + total[8:16] + total[16:24]) * np.float32(1.0 / (C * LON * SUMW))
    flat = iota((8, 128), 0) * 128 + iota((8, 128), 1)
    channel = lax.shift_right_logical(flat * 2731, 16)
    weight = row_weight(lat_index() * ROWS + flat - channel * ROWS)
    inv = jnp.zeros((8, 128), F32)
    for c in range(C):
        inv = jnp.where(channel == c, inverse_square(scales_ref, c), inv)
    aux_ref[8:16] = weight * inv * np.float32(1.0 / (C * SUMW * GROUP))


def distance_kernel(scales_ref, recv_ref, aux_ref, msg_ref, zall_ref, rows_ref):
    me = lax.axis_index("y")
    inv = inverse_square(scales_ref, me * 2 + lax.axis_index("xl"))
    w = tile_weights((ROWS, 128)) * (inv * np.float32(1.0 / (C * LON * SUMW)))
    row, lane = iota((8, 128), 0), iota((8, 128), 1)
    got = [recv_ref[s].astype(F32) for s in range(GROUP)]
    rows_ref[...] = jnp.zeros((128, 128), F32)
    pairs = [(k, m, (m - k) % M) for k in (1, 2, 3, 4) for m in range(M) if k < 4 or m < 4]

    def put(at, value):
        rows_ref[at : at + 1] = jnp.sum(value, axis=0, keepdims=True)

    totals = [jnp.zeros((8, 128), F32) for _ in pairs]
    for t in range(3):
        rows8 = slice(t * 8, t * 8 + 8)
        for p, (_, m, n) in enumerate(pairs):
            acc = None
            for l in range(4):
                d = got[m * 4 + l][rows8] - got[n * 4 + l][rows8]
                acc = d * d if acc is None else acc + d * d
            totals[p] = totals[p] + acc * w[rows8]
    for p, (k, m, _) in enumerate(pairs):
        put((k - 1) * 8 + m, totals[p])
    rows_ref[32:40] = jnp.where(row == me, jnp.sum(aux_ref[0:8], axis=0, keepdims=True), 0.0)

    zw = aux_ref[8:16]
    real = row < 3
    zobs = jnp.zeros((8, 128), F32)
    zonal = []
    for m in range(M):
        s = sum(got[m * 4 + l][24:32] for l in range(4))
        z = jnp.where(real, s + jnp.concatenate([s[3:8], s[0:3]], axis=0), 0.0) * np.float32(1.0 / LON)
        zonal.append(z)
        zall_ref[m] = z
        part = s[6:7] + s[7:8]
        zobs = jnp.where(real & part_of(m, row, lane), part, zobs)
    zobs = zobs * np.float32(1.0 / LON)
    zall_ref[M] = zobs
    for k, m, n in pairs:
        d = zonal[m] - zonal[n]
        put(40 + (k - 1) * 8 + m, zw * d * d)
    for m in range(M):
        d = zonal[m] - zobs
        put(72 + m, zw * d * d)
    ones = jnp.ones((8, 128), F32)
    sums = lax.dot_general(
        ones, rows_ref[...], (((1,), (1,)), ((), ())), precision=HIGHEST, preferred_element_type=F32
    )
    for i in range(msg_ref.shape[0]):
        msg_ref[i] = sums[0:1]


def relay_kernel(in_ref, out_ref):
    total = jnp.sum(in_ref[...], axis=0)
    out_ref[...] = jnp.broadcast_to(total[None], out_ref.shape)


def mix_kernel(scales_ref, msg_ref, zall_ref, gat_ref, obs_ref, out_ref, coef_ref, zcol_ref):
    me = lax.axis_index("y")
    step = pl.program_id(0)
    per = out_ref.shape[1]

    @pl.when(step == 0)
    def _():
        dist = jnp.sum(msg_ref[...], axis=0)
        row, lane = iota((16, 128), 0), iota((16, 128), 1)
        j = row & 7
        k = j + 1
        at = jnp.where(
            k <= 3,
            j * 8 + ((me + k) & 7),
            jnp.where(k == 4, 24 + (me & 3), jnp.where(k <= 7, (7 - k) * 8 + me, 32 + me)),
        )
        at = at + jnp.where(row >= 8, 40, 0)
        e = jnp.broadcast_to(jnp.exp(dist * np.float32(-0.5 / BAND)), (16, 128))
        picked = jnp.sum(jnp.where(lane == at, e, 0.0), axis=1, keepdims=True)
        norm = jnp.where(row == 7, 1.0 / (M * BAND), jnp.where(row == 15, 1.0 / (M * BAND), 1.0 / (M * (M - 1) * BAND)))
        coef = jnp.broadcast_to(picked, (16, 128)) * norm
        coef_ref[...] = coef
        zme = zall_ref[me]
        z = coef[15:16] * (zme - zall_ref[M])
        for k in range(1, M):
            z = z + coef[7 + k : 8 + k] * (zall_ref[(me + k) & 7] - zme)
        for b in range(3):
            zcol_ref[b * 128 : (b + 1) * 128] = jnp.broadcast_to(z[b : b + 1], (128, 128)).T

    fac = tile_weights((ROWS, COLS)) * np.float32(LAT / SUMW)
    coef = coef_ref[...]
    own_b = coef[7:8]
    for i in range(per):
        c = step * per + i
        xm = gat_ref[me, i].astype(F32)
        acc = jnp.concatenate([own_b, own_b], axis=1) * (xm - obs_ref[i].astype(F32))
        for k in range(1, M):
            a = coef[k - 1 : k]
            acc = acc + jnp.concatenate([a, a], axis=1) * (gat_ref[(me + k) & 7, i].astype(F32) - xm)
        z = zcol_ref[pl.ds(pl.multiple_of(c * ROWS, 8), ROWS)]
        acc = acc + jnp.concatenate([z, z], axis=1)
        out_ref[0, i] = acc * (fac * inverse_square(scales_ref, c))


VMEM = pl.BlockSpec(memory_space=pltpu.VMEM)
SMEM = pl.BlockSpec(memory_space=pltpu.SMEM)


def call(kernel, out_shape, in_specs, cost, **kw):
    return pl.pallas_call(
        kernel,
        out_shape=out_shape,
        in_specs=in_specs,
        cost_estimate=pl.CostEstimate(flops=cost, bytes_accessed=cost, transcendentals=0),
        compiler_params=pltpu.CompilerParams(vmem_limit_bytes=32 * 1024 * 1024),
        **kw,
    )


def per_device(members, observed, scales):
    shape = jax.ShapeDtypeStruct
    gathered = lax.all_gather(members, "y", axis=0, tiled=True)
    pay = call(pack_kernel, shape((GROUP, 32, 128), BF16), [VMEM] * 2, 1 << 20, out_specs=VMEM)(members, observed)
    aux = call(local_kernel, shape((16, 128), F32), [SMEM, VMEM, VMEM], 1 << 20, out_specs=VMEM)(
        scales, members, observed
    )
    recv = lax.all_to_all(pay, ("y", "xl", "core"), 0, 0, tiled=True)
    msg, zall = call(
        distance_kernel,
        (shape((16, 1, 128), F32), shape((16, 8, 128), F32)),
        [SMEM, VMEM, VMEM],
        1 << 20,
        out_specs=(VMEM, VMEM),
        scratch_shapes=[pltpu.VMEM((128, 128), F32)],
    )(scales, recv, aux)
    msg = lax.all_to_all(msg, ("xh", "xl", "core"), 0, 0, tiled=True)
    msg = call(relay_kernel, shape((64, 1, 128), F32), [VMEM], 1 << 16, out_specs=VMEM)(msg)
    msg = lax.all_to_all(msg, ("y", "z"), 0, 0, tiled=True)
    steps = 4
    per = C // steps
    return call(
        mix_kernel,
        shape((1, C, ROWS, COLS), F32),
        [
            SMEM,
            pl.BlockSpec((64, 1, 128), lambda i: (0, 0, 0)),
            pl.BlockSpec((16, 8, 128), lambda i: (0, 0, 0)),
            pl.BlockSpec((M, per, ROWS, COLS), lambda i: (0, i, 0, 0)),
            pl.BlockSpec((per, ROWS, COLS), lambda i: (i, 0, 0)),
        ],
        1 << 22,
        grid=(steps,),
        out_specs=pl.BlockSpec((1, per, ROWS, COLS), lambda i: (0, i, 0, 0)),
        scratch_shapes=[pltpu.VMEM((16, 128), F32), pltpu.VMEM((CELLS, 128), F32)],
    )(scales, msg, zall, gathered, observed)


def solution(mesh):
    fine = Mesh(mesh.devices.reshape(8, 8, 4, 2, 2), ("y", "z", "xh", "xl", "core"))
    placed = P("y", None, ("z", "xh"), ("xl", "core"))
    return jax.shard_map(
        per_device,
        mesh=fine,
        in_specs=(placed, P(None, ("z", "xh"), ("xl", "core")), P()),
        out_specs=placed,
        check_vma=False,
    )
```

```python
import functools

import jax
import jax.numpy as jnp
import numpy as np
from jax import lax
from jax.experimental import pallas as pl
from jax.experimental.pallas import tpu as pltpu
from jax.sharding import Mesh
from jax.sharding import PartitionSpec as P

BAND = 1.0
F32 = jnp.float32
BF16 = jnp.bfloat16
C, M, LAT, LON = 16, 8, 768, 1024
ROWS, COLS = 24, 256
CELLS = C * ROWS
PARTS = 8
GROUP = 32
LONG = 1 << 36
HIGHEST = lax.Precision.HIGHEST


def total_weight():
    index = np.arange(LAT).astype(np.float32)
    angle = (np.float32(-90.0) + (index + np.float32(0.5)) * np.float32(180.0) / np.float32(LAT)) * np.float32(
        np.pi / 180.0
    )
    return float(np.sum(np.cos(angle.astype(np.float32)).astype(np.float64)))


SUMW = total_weight()


def row_weight(index):
    angle = (-90.0 + (index.astype(F32) + 0.5) * 180.0 / LAT) * np.float32(np.pi / 180.0)
    return jnp.cos(angle)


def iota(shape, axis):
    return lax.broadcasted_iota(jnp.int32, shape, axis)


def lat_index():
    return lax.axis_index("z") * 4 + lax.axis_index("xh")


def tile_weights(shape):
    return row_weight(lat_index() * ROWS + iota(shape, 0))


def inverse_square(scales_ref, c):
    s = scales_ref[c]
    return 1.0 / (s * s)


def lanes_sum(x):
    ones = jnp.ones((8, COLS), BF16)
    flat = x.reshape(CELLS, COLS).astype(BF16)
    return lax.dot_general(ones, flat, (((1,), (1,)), ((), ())), preferred_element_type=F32)


def part_of(part, block, lane):
    flat = block * 128 + lane
    return (flat >= part * (CELLS // M)) & (flat < (part + 1) * (CELLS // M))


def pack_kernel(own_hbm, obs_hbm, pay_ref, own_ref, obs_ref, sems):
    me = lax.axis_index("y")
    get_own = pltpu.make_async_copy(own_hbm, own_ref, sems.at[0])
    get_obs = pltpu.make_async_copy(obs_hbm, obs_ref, sems.at[1])
    get_own.start()
    get_obs.start()
    get_own.wait()
    x = own_ref[0].astype(F32)
    zx = lanes_sum(x)
    get_obs.wait()
    zy = lanes_sum(obs_ref[...].astype(F32))
    row, lane = iota((8, 128), 0), iota((8, 128), 1)

    def high(v):
        return v.astype(BF16).astype(F32)

    part = jnp.zeros((8, 128), F32)
    extra = jnp.zeros((8, 128), F32)
    for k in range(3):
        part = jnp.where(part_of(me, k, lane), zy[:, k * 128 : (k + 1) * 128], part)
        zk = zx[:, k * 128 : (k + 1) * 128]
        extra = jnp.where(row == k, high(zk), extra)
        extra = jnp.where(row == k + 3, zk - high(zk), extra)
    extra = jnp.where(row == 6, high(part), extra)
    extra = jnp.where(row == 7, part - high(part), extra)
    for d in range(GROUP):
        h = d % 2
        pay_ref[d] = jnp.concatenate([x[d // 2, :, h * 128 : (h + 1) * 128], extra], axis=0).astype(BF16)


def local_kernel(scales_ref, own_ref, obs_ref, pay_ref, aux_ref, copy_ref):
    copy_ref[...] = own_ref[0]
    w = tile_weights((ROWS, 128))
    total = jnp.zeros((ROWS, 128), F32)
    for c in range(C):
        d = own_ref[0, c].astype(F32) - obs_ref[c].astype(F32)
        d = d * d
        total = total + (d[:, :128] + d[:, 128:]) * inverse_square(scales_ref, c)
    total = total * w
    aux_ref[0:8] = (total[0:8] + total[8:16] + total[16:24]) * np.float32(1.0 / (C * LON * SUMW))
    flat = iota((8, 128), 0) * 128 + iota((8, 128), 1)
    channel = lax.shift_right_logical(flat * 2731, 16)
    weight = row_weight(lat_index() * ROWS + flat - channel * ROWS)
    inv = jnp.zeros((8, 128), F32)
    for c in range(C):
        inv = jnp.where(channel == c, inverse_square(scales_ref, c), inv)
    aux_ref[8:16] = weight * inv * np.float32(1.0 / (C * SUMW * GROUP))


def distance_kernel(scales_ref, recv_ref, aux_ref, msg_ref, zall_ref, rows_ref):
    me = lax.axis_index("y")
    inv = inverse_square(scales_ref, me * 2 + lax.axis_index("xl"))
    w = tile_weights((ROWS, 128)) * (inv * np.float32(1.0 / (C * LON * SUMW)))
    row, lane = iota((8, 128), 0), iota((8, 128), 1)
    got = [recv_ref[s].astype(F32) for s in range(GROUP)]
    rows_ref[...] = jnp.zeros((128, 128), F32)
    pairs = [(k, m, (m - k) % M) for k in (1, 2, 3, 4) for m in range(M) if k < 4 or m < 4]

    def put(at, value):
        rows_ref[at : at + 1] = jnp.sum(value, axis=0, keepdims=True)

    totals = [jnp.zeros((8, 128), F32) for _ in pairs]
    for t in range(3):
        rows8 = slice(t * 8, t * 8 + 8)
        for p, (_, m, n) in enumerate(pairs):
            acc = None
            for l in range(4):
                d = got[m * 4 + l][rows8] - got[n * 4 + l][rows8]
                acc = d * d if acc is None else acc + d * d
            totals[p] = totals[p] + acc * w[rows8]
    for p, (k, m, _) in enumerate(pairs):
        put((k - 1) * 8 + m, totals[p])
    rows_ref[32:40] = jnp.where(row == me, jnp.sum(aux_ref[0:8], axis=0, keepdims=True), 0.0)

    zw = aux_ref[8:16]
    real = row < 3
    zobs = jnp.zeros((8, 128), F32)
    zonal = []
    for m in range(M):
        s = sum(got[m * 4 + l][24:32] for l in range(4))
        z = jnp.where(real, s + jnp.concatenate([s[3:8], s[0:3]], axis=0), 0.0) * np.float32(1.0 / LON)
        zonal.append(z)
        zall_ref[m] = z
        part = s[6:7] + s[7:8]
        zobs = jnp.where(real & part_of(m, row, lane), part, zobs)
    zobs = zobs * np.float32(1.0 / LON)
    zall_ref[M] = zobs
    for k, m, n in pairs:
        d = zonal[m] - zonal[n]
        put(40 + (k - 1) * 8 + m, zw * d * d)
    for m in range(M):
        d = zonal[m] - zobs
        put(72 + m, zw * d * d)
    ones = jnp.ones((8, 128), F32)
    sums = lax.dot_general(
        ones, rows_ref[...], (((1,), (1,)), ((), ())), precision=HIGHEST, preferred_element_type=F32
    )
    for i in range(msg_ref.shape[0]):
        msg_ref[i] = sums[0:1]


def relay_kernel(in_ref, out_ref):
    total = jnp.sum(in_ref[...], axis=0)
    out_ref[...] = jnp.broadcast_to(total[None], out_ref.shape)


def after_kernel(*refs):
    pass


def coefficient_kernel(msg_ref, zall_ref, coef_ref, zcol_ref):
    me = lax.axis_index("y")
    dist = jnp.sum(msg_ref[...], axis=0)
    row, lane = iota((16, 128), 0), iota((16, 128), 1)
    j = row & 7
    k = j + 1
    at = jnp.where(
        k <= 3,
        j * 8 + ((me + k) & 7),
        jnp.where(k == 4, 24 + (me & 3), jnp.where(k <= 7, (7 - k) * 8 + me, 32 + me)),
    )
    at = at + jnp.where(row >= 8, 40, 0)
    e = jnp.broadcast_to(jnp.exp(dist * np.float32(-0.5 / BAND)), (16, 128))
    picked = jnp.sum(jnp.where(lane == at, e, 0.0), axis=1, keepdims=True)
    norm = jnp.where(j == 7, 1.0 / (M * BAND), 1.0 / (M * (M - 1) * BAND))
    coef = jnp.broadcast_to(picked, (16, 128)) * norm
    coef_ref[...] = coef
    zme = zall_ref[me]
    z = coef[15:16] * (zme - zall_ref[M])
    for k in range(1, M):
        z = z + coef[7 + k : 8 + k] * (zall_ref[(me + k) & 7] - zme)
    for b in range(3):
        zcol_ref[b * 128 : (b + 1) * 128] = jnp.broadcast_to(z[b : b + 1], (128, 128)).T


def mix_kernel(scales_ref, coef_ref, zcol_ref, obs_ref, *refs):
    tiles, (out_hbm, out_ref, sems) = refs[:M], refs[M:]
    fac = tile_weights((ROWS, COLS)) * np.float32(LAT / SUMW)
    coef = coef_ref[...]
    coef = jnp.concatenate([coef, coef], axis=1)
    per = C // PARTS
    copies = []
    for c in range(C):
        xm = tiles[0][c].astype(F32)
        acc = coef[7:8] * (xm - obs_ref[c].astype(F32))
        for k in range(1, M):
            acc = acc + coef[k - 1 : k] * (tiles[k][c].astype(F32) - xm)
        z = zcol_ref[c * ROWS : (c + 1) * ROWS]
        acc = acc + jnp.concatenate([z, z], axis=1)
        out_ref[c] = acc * (fac * inverse_square(scales_ref, c))
        if c % per == per - 1:
            part = pl.ds(c + 1 - per, per)
            copies.append(pltpu.make_async_copy(out_ref.at[part], out_hbm.at[0, part], sems.at[c // per]))
            copies[-1].start()
    for copy in copies:
        copy.wait()


VMEM = pl.BlockSpec(memory_space=pltpu.VMEM)
SMEM = pl.BlockSpec(memory_space=pltpu.SMEM)


def call(kernel, out_shape, in_specs, cost, vmem=32, **kw):
    return pl.pallas_call(
        kernel,
        out_shape=out_shape,
        in_specs=in_specs,
        cost_estimate=pl.CostEstimate(flops=cost, bytes_accessed=cost, transcendentals=0),
        compiler_params=pltpu.CompilerParams(vmem_limit_bytes=vmem * 1024 * 1024),
        **kw,
    )


def after(arrays, made):
    spec = pl.BlockSpec(memory_space=pl.ANY)
    return call(
        after_kernel,
        [jax.ShapeDtypeStruct(a.shape, a.dtype) for a in arrays],
        [spec] * (len(arrays) + 1),
        1 << 22,
        out_specs=[spec] * len(arrays),
        input_output_aliases={i: i for i in range(len(arrays))},
    )(*arrays, made)


def from_ahead(tile, k):
    return lax.ppermute(tile, "y", [((i + k) % M, i) for i in range(M)])


def per_device(members, observed, scales):
    shape = jax.ShapeDtypeStruct
    tile = shape((C, ROWS, COLS), BF16)
    anywhere = pl.BlockSpec(memory_space=pl.ANY)
    hbm = pl.BlockSpec(memory_space=pltpu.HBM)
    pay = call(
        pack_kernel,
        shape((GROUP, 32, 128), BF16),
        [hbm] * 2,
        1 << 20,
        vmem=60,
        out_specs=VMEM,
        scratch_shapes=[
            pltpu.VMEM((1, C, ROWS, COLS), BF16),
            pltpu.VMEM((C, ROWS, COLS), BF16),
            pltpu.SemaphoreType.DMA((2,)),
        ],
    )(members, observed)
    aux, own = call(
        local_kernel, (shape((16, 128), F32), tile), [SMEM, VMEM, VMEM, anywhere], 1 << 20, out_specs=(VMEM, VMEM)
    )(scales, members, observed, pay)
    tiles = [own] + [None] * 7
    recv = lax.all_to_all(pay, ("y", "xl", "core"), 0, 0, tiled=True)
    tiles[1], tiles[7] = from_ahead(own, 1), from_ahead(own, -1)
    msg, zall = call(
        distance_kernel,
        (shape((16, 1, 128), F32), shape((16, 8, 128), F32)),
        [SMEM, VMEM, VMEM],
        LONG,
        out_specs=(VMEM, VMEM),
        scratch_shapes=[pltpu.VMEM((128, 128), F32)],
    )(scales, recv, aux)
    tiles[1], tiles[7] = after([tiles[1], tiles[7]], msg)
    msg = lax.all_to_all(msg, ("xh", "xl", "core"), 0, 0, tiled=True)
    tiles[2], tiles[6] = from_ahead(tiles[1], 1), from_ahead(tiles[7], -1)
    msg = call(relay_kernel, shape((64, 1, 128), F32), [VMEM], LONG, out_specs=VMEM)(msg)
    tiles[2], tiles[6] = after([tiles[2], tiles[6]], msg)
    msg = lax.all_to_all(msg, ("y", "z"), 0, 0, tiled=True)
    tiles[3], tiles[5], tiles[4] = from_ahead(tiles[2], 1), from_ahead(tiles[6], -1), from_ahead(tiles[2], 2)
    coef, zcol = call(
        coefficient_kernel,
        (shape((16, 128), F32), shape((CELLS, 128), F32)),
        [VMEM] * 2,
        LONG,
        out_specs=(VMEM, VMEM),
    )(msg, zall)
    return call(
        mix_kernel,
        shape((1, C, ROWS, COLS), F32),
        [SMEM] + [VMEM] * (3 + M),
        1 << 22,
        out_specs=hbm,
        scratch_shapes=[pltpu.VMEM((C, ROWS, COLS), F32), pltpu.SemaphoreType.DMA((PARTS,))],
    )(scales, coef, zcol, observed, *tiles)


def solution(mesh):
    fine = Mesh(mesh.devices.reshape(8, 8, 4, 2, 2), ("y", "z", "xh", "xl", "core"))
    placed = P("y", None, ("z", "xh"), ("xl", "core"))
    return jax.shard_map(
        per_device,
        mesh=fine,
        in_specs=(placed, P(None, ("z", "xh"), ("xl", "core")), P()),
        out_specs=placed,
        check_vma=False,
    )
```

```python
import functools

import jax
import jax.numpy as jnp
import numpy as np
from jax import lax
from jax.experimental import pallas as pl
from jax.experimental.pallas import tpu as pltpu
from jax.sharding import Mesh
from jax.sharding import PartitionSpec as P

BAND = 1.0
F32 = jnp.float32
BF16 = jnp.bfloat16
C, M, LAT, LON = 16, 8, 768, 1024
ROWS, COLS = 24, 256
CELLS = C * ROWS
PARTS = 8
GROUP = 32
LONG = 1 << 36
HIGHEST = lax.Precision.HIGHEST


def total_weight():
    index = np.arange(LAT).astype(np.float32)
    angle = (np.float32(-90.0) + (index + np.float32(0.5)) * np.float32(180.0) / np.float32(LAT)) * np.float32(
        np.pi / 180.0
    )
    return float(np.sum(np.cos(angle.astype(np.float32)).astype(np.float64)))


SUMW = total_weight()


def row_weight(index):
    angle = (-90.0 + (index.astype(F32) + 0.5) * 180.0 / LAT) * np.float32(np.pi / 180.0)
    return jnp.cos(angle)


def iota(shape, axis):
    return lax.broadcasted_iota(jnp.int32, shape, axis)


def lat_index():
    return lax.axis_index("z") * 4 + lax.axis_index("xh")


def tile_weights(shape):
    return row_weight(lat_index() * ROWS + iota(shape, 0))


def inverse_square(scales_ref, c):
    s = scales_ref[c]
    return 1.0 / (s * s)


def lanes_sum(x):
    ones = jnp.ones((8, COLS), BF16)
    flat = x.reshape(CELLS, COLS).astype(BF16)
    return lax.dot_general(ones, flat, (((1,), (1,)), ((), ())), preferred_element_type=F32)


def part_of(part, block, lane):
    flat = block * 128 + lane
    return (flat >= part * (CELLS // M)) & (flat < (part + 1) * (CELLS // M))


def fill_local(scales_ref, x, y, aux_ref):
    w = tile_weights((ROWS, 128))
    total = jnp.zeros((ROWS, 128), F32)
    for c in range(C):
        d = x[c] - y[c]
        d = d * d
        total = total + (d[:, :128] + d[:, 128:]) * inverse_square(scales_ref, c)
    total = total * w
    aux_ref[0:8] = (total[0:8] + total[8:16] + total[16:24]) * np.float32(1.0 / (C * LON * SUMW))
    flat = iota((8, 128), 0) * 128 + iota((8, 128), 1)
    channel = lax.shift_right_logical(flat * 2731, 16)
    weight = row_weight(lat_index() * ROWS + flat - channel * ROWS)
    inv = jnp.zeros((8, 128), F32)
    for c in range(C):
        inv = jnp.where(channel == c, inverse_square(scales_ref, c), inv)
    aux_ref[8:16] = weight * inv * np.float32(1.0 / (C * SUMW * GROUP))


def pack_kernel(scales_ref, own_hbm, obs_hbm, pay_ref, aux_ref, own_ref, obs_ref, sems):
    me = lax.axis_index("y")
    get_own = pltpu.make_async_copy(own_hbm, own_ref, sems.at[0])
    get_obs = pltpu.make_async_copy(obs_hbm, obs_ref, sems.at[1])
    get_own.start()
    get_obs.start()
    get_own.wait()
    x = own_ref[0].astype(F32)
    zx = lanes_sum(x)
    get_obs.wait()
    y = obs_ref[...].astype(F32)
    zy = lanes_sum(y)
    fill_local(scales_ref, x, y, aux_ref)
    row, lane = iota((8, 128), 0), iota((8, 128), 1)

    def high(v):
        return v.astype(BF16).astype(F32)

    part = jnp.zeros((8, 128), F32)
    extra = jnp.zeros((8, 128), F32)
    for k in range(3):
        part = jnp.where(part_of(me, k, lane), zy[:, k * 128 : (k + 1) * 128], part)
        zk = zx[:, k * 128 : (k + 1) * 128]
        extra = jnp.where(row == k, high(zk), extra)
        extra = jnp.where(row == k + 3, zk - high(zk), extra)
    extra = jnp.where(row == 6, high(part), extra)
    extra = jnp.where(row == 7, part - high(part), extra)
    for d in range(GROUP):
        h = d % 2
        pay_ref[d] = jnp.concatenate([x[d // 2, :, h * 128 : (h + 1) * 128], extra], axis=0).astype(BF16)


def distance_kernel(scales_ref, recv_ref, aux_ref, msg_ref, zall_ref, token_ref, rows_ref):
    token_ref[...] = jnp.zeros((8, 128), F32)
    me = lax.axis_index("y")
    inv = inverse_square(scales_ref, me * 2 + lax.axis_index("xl"))
    w = tile_weights((ROWS, 128)) * (inv * np.float32(1.0 / (C * LON * SUMW)))
    row, lane = iota((8, 128), 0), iota((8, 128), 1)
    got = [recv_ref[s].astype(F32) for s in range(GROUP)]
    rows_ref[...] = jnp.zeros((128, 128), F32)
    pairs = [(k, m, (m - k) % M) for k in (1, 2, 3, 4) for m in range(M) if k < 4 or m < 4]

    def put(at, value):
        rows_ref[at : at + 1] = jnp.sum(value, axis=0, keepdims=True)

    totals = [jnp.zeros((8, 128), F32) for _ in pairs]
    for t in range(3):
        rows8 = slice(t * 8, t * 8 + 8)
        for p, (_, m, n) in enumerate(pairs):
            acc = None
            for l in range(4):
                d = got[m * 4 + l][rows8] - got[n * 4 + l][rows8]
                acc = d * d if acc is None else acc + d * d
            totals[p] = totals[p] + acc * w[rows8]
    for p, (k, m, _) in enumerate(pairs):
        put((k - 1) * 8 + m, totals[p])
    rows_ref[32:40] = jnp.where(row == me, jnp.sum(aux_ref[0:8], axis=0, keepdims=True), 0.0)

    zw = aux_ref[8:16]
    real = row < 3
    zobs = jnp.zeros((8, 128), F32)
    zonal = []
    for m in range(M):
        s = sum(got[m * 4 + l][24:32] for l in range(4))
        z = jnp.where(real, s + jnp.concatenate([s[3:8], s[0:3]], axis=0), 0.0) * np.float32(1.0 / LON)
        zonal.append(z)
        zall_ref[m] = z
        part = s[6:7] + s[7:8]
        zobs = jnp.where(real & part_of(m, row, lane), part, zobs)
    zobs = zobs * np.float32(1.0 / LON)
    zall_ref[M] = zobs
    for k, m, n in pairs:
        d = zonal[m] - zonal[n]
        put(40 + (k - 1) * 8 + m, zw * d * d)
    for m in range(M):
        d = zonal[m] - zobs
        put(72 + m, zw * d * d)
    ones = jnp.ones((8, 128), F32)
    sums = lax.dot_general(
        ones, rows_ref[...], (((1,), (1,)), ((), ())), precision=HIGHEST, preferred_element_type=F32
    )
    for i in range(msg_ref.shape[0]):
        msg_ref[i] = sums[0:1]


def relay_kernel(in_ref, out_ref):
    total = jnp.sum(in_ref[...], axis=0)
    out_ref[...] = jnp.broadcast_to(total[None], out_ref.shape)


def after_kernel(*refs):
    pass


def coefficient_kernel(msg_ref, zall_ref, coef_ref, zcol_ref):
    me = lax.axis_index("y")
    dist = jnp.sum(msg_ref[...], axis=0)
    row, lane = iota((16, 128), 0), iota((16, 128), 1)
    j = row & 7
    k = j + 1
    at = jnp.where(
        k <= 3,
        j * 8 + ((me + k) & 7),
        jnp.where(k == 4, 24 + (me & 3), jnp.where(k <= 7, (7 - k) * 8 + me, 32 + me)),
    )
    at = at + jnp.where(row >= 8, 40, 0)
    e = jnp.broadcast_to(jnp.exp(dist * np.float32(-0.5 / BAND)), (16, 128))
    picked = jnp.sum(jnp.where(lane == at, e, 0.0), axis=1, keepdims=True)
    norm = jnp.where(j == 7, 1.0 / (M * BAND), 1.0 / (M * (M - 1) * BAND))
    coef = jnp.broadcast_to(picked, (16, 128)) * norm
    coef_ref[...] = coef
    zme = zall_ref[me]
    z = coef[15:16] * (zme - zall_ref[M])
    for k in range(1, M):
        z = z + coef[7 + k : 8 + k] * (zall_ref[(me + k) & 7] - zme)
    for b in range(3):
        zcol_ref[b * 128 : (b + 1) * 128] = jnp.broadcast_to(z[b : b + 1], (128, 128)).T


def mix_kernel(scales_ref, coef_ref, zcol_ref, obs_ref, *refs):
    tiles, (out_hbm, out_ref, sems) = refs[:M], refs[M:]
    fac = tile_weights((ROWS, COLS)) * np.float32(LAT / SUMW)
    coef = coef_ref[...]
    coef = jnp.concatenate([coef, coef], axis=1)
    per = C // PARTS
    copies = []
    for c in range(C):
        xm = tiles[0][c].astype(F32)
        acc = coef[7:8] * (xm - obs_ref[c].astype(F32))
        for k in range(1, M):
            acc = acc + coef[k - 1 : k] * (tiles[k][c].astype(F32) - xm)
        z = zcol_ref[c * ROWS : (c + 1) * ROWS]
        acc = acc + jnp.concatenate([z, z], axis=1)
        out_ref[c] = acc * (fac * inverse_square(scales_ref, c))
        if c % per == per - 1:
            part = pl.ds(c + 1 - per, per)
            copies.append(pltpu.make_async_copy(out_ref.at[part], out_hbm.at[0, part], sems.at[c // per]))
            copies[-1].start()
    for copy in copies:
        copy.wait()


VMEM = pl.BlockSpec(memory_space=pltpu.VMEM)
SMEM = pl.BlockSpec(memory_space=pltpu.SMEM)


def call(kernel, out_shape, in_specs, cost, vmem=32, **kw):
    return pl.pallas_call(
        kernel,
        out_shape=out_shape,
        in_specs=in_specs,
        cost_estimate=pl.CostEstimate(flops=cost, bytes_accessed=cost, transcendentals=0),
        compiler_params=pltpu.CompilerParams(vmem_limit_bytes=vmem * 1024 * 1024),
        **kw,
    )


def after(arrays, made):
    spec = pl.BlockSpec(memory_space=pl.ANY)
    return call(
        after_kernel,
        [jax.ShapeDtypeStruct(a.shape, a.dtype) for a in arrays],
        [spec] * len(arrays) + [VMEM],
        1 << 22,
        out_specs=[spec] * len(arrays),
        input_output_aliases={i: i for i in range(len(arrays))},
    )(*arrays, made)


def from_ahead(tile, k):
    return lax.ppermute(tile, "y", [((i + k) % M, i) for i in range(M)])


def per_device(members, observed, scales):
    shape = jax.ShapeDtypeStruct
    hbm = pl.BlockSpec(memory_space=pltpu.HBM)
    pay, aux = call(
        pack_kernel,
        (shape((GROUP, 32, 128), BF16), shape((16, 128), F32)),
        [SMEM, hbm, hbm],
        1 << 20,
        vmem=60,
        out_specs=(VMEM, VMEM),
        scratch_shapes=[
            pltpu.VMEM((1, C, ROWS, COLS), BF16),
            pltpu.VMEM((C, ROWS, COLS), BF16),
            pltpu.SemaphoreType.DMA((2,)),
        ],
    )(scales, members, observed)
    tiles = [members[0]] + [None] * 7
    tiles[1], tiles[7] = from_ahead(tiles[0], 1), from_ahead(tiles[0], -1)
    recv = lax.all_to_all(pay, ("y", "xl", "core"), 0, 0, tiled=True)
    tiles[2], tiles[6] = from_ahead(tiles[0], 2), from_ahead(tiles[0], -2)
    msg, zall, token = call(
        distance_kernel,
        (shape((16, 1, 128), F32), shape((16, 8, 128), F32), shape((8, 128), F32)),
        [SMEM, VMEM, VMEM],
        LONG,
        out_specs=(VMEM, VMEM, VMEM),
        scratch_shapes=[pltpu.VMEM((128, 128), F32)],
    )(scales, recv, aux)
    msg = lax.all_to_all(msg, ("xh", "xl", "core"), 0, 0, tiled=True)
    tiles[1], tiles[2], tiles[6], tiles[7] = after([tiles[1], tiles[2], tiles[6], tiles[7]], token)
    tiles[3], tiles[5], tiles[4] = from_ahead(tiles[2], 1), from_ahead(tiles[6], -1), from_ahead(tiles[2], 2)
    msg = call(relay_kernel, shape((64, 1, 128), F32), [VMEM], LONG, out_specs=VMEM)(msg)
    msg = lax.all_to_all(msg, ("y", "z"), 0, 0, tiled=True)
    coef, zcol = call(
        coefficient_kernel,
        (shape((16, 128), F32), shape((CELLS, 128), F32)),
        [VMEM] * 2,
        1 << 16,
        out_specs=(VMEM, VMEM),
    )(msg, zall)
    return call(
        mix_kernel,
        shape((1, C, ROWS, COLS), F32),
        [SMEM] + [VMEM] * (3 + M),
        1 << 22,
        out_specs=hbm,
        scratch_shapes=[pltpu.VMEM((C, ROWS, COLS), F32), pltpu.SemaphoreType.DMA((PARTS,))],
    )(scales, coef, zcol, observed, *tiles)


def solution(mesh):
    fine = Mesh(mesh.devices.reshape(8, 8, 4, 2, 2), ("y", "z", "xh", "xl", "core"))
    placed = P("y", None, ("z", "xh"), ("xl", "core"))
    return jax.shard_map(
        per_device,
        mesh=fine,
        in_specs=(placed, P(None, ("z", "xh"), ("xl", "core")), P()),
        out_specs=placed,
        check_vma=False,
    )
```

```python
import functools

import jax
import jax.numpy as jnp
import numpy as np
from jax import lax
from jax.experimental import pallas as pl
from jax.experimental.pallas import tpu as pltpu
from jax.sharding import Mesh
from jax.sharding import PartitionSpec as P

BAND = 1.0
F32 = jnp.float32
BF16 = jnp.bfloat16
C, M, LAT, LON = 16, 8, 768, 1024
ROWS, COLS = 24, 256
CELLS = C * ROWS
PARTS = 8
GROUP = 32
LONG = 1 << 36
HIGHEST = lax.Precision.HIGHEST


def total_weight():
    index = np.arange(LAT).astype(np.float32)
    angle = (np.float32(-90.0) + (index + np.float32(0.5)) * np.float32(180.0) / np.float32(LAT)) * np.float32(
        np.pi / 180.0
    )
    return float(np.sum(np.cos(angle.astype(np.float32)).astype(np.float64)))


SUMW = total_weight()


def row_weight(index):
    angle = (-90.0 + (index.astype(F32) + 0.5) * 180.0 / LAT) * np.float32(np.pi / 180.0)
    return jnp.cos(angle)


def iota(shape, axis):
    return lax.broadcasted_iota(jnp.int32, shape, axis)


def lat_index():
    return lax.axis_index("z") * 4 + lax.axis_index("xh")


def tile_weights(shape):
    return row_weight(lat_index() * ROWS + iota(shape, 0))


def inverse_square(scales_ref, c):
    s = scales_ref[c]
    return 1.0 / (s * s)


def lanes_sum(x):
    ones = jnp.ones((8, COLS), BF16)
    flat = x.reshape(CELLS, COLS).astype(BF16)
    return lax.dot_general(ones, flat, (((1,), (1,)), ((), ())), preferred_element_type=F32)


def part_of(part, block, lane):
    flat = block * 128 + lane
    return (flat >= part * (CELLS // M)) & (flat < (part + 1) * (CELLS // M))


def fill_local(scales_ref, x, y, aux_ref):
    w = tile_weights((ROWS, 128))
    total = jnp.zeros((ROWS, 128), F32)
    for c in range(C):
        d = x[c] - y[c]
        d = d * d
        total = total + (d[:, :128] + d[:, 128:]) * inverse_square(scales_ref, c)
    total = total * w
    aux_ref[0:8] = (total[0:8] + total[8:16] + total[16:24]) * np.float32(1.0 / (C * LON * SUMW))
    flat = iota((8, 128), 0) * 128 + iota((8, 128), 1)
    channel = lax.shift_right_logical(flat * 2731, 16)
    weight = row_weight(lat_index() * ROWS + flat - channel * ROWS)
    inv = jnp.zeros((8, 128), F32)
    for c in range(C):
        inv = jnp.where(channel == c, inverse_square(scales_ref, c), inv)
    aux_ref[8:16] = weight * inv * np.float32(1.0 / (C * SUMW * GROUP))


def pack_kernel(scales_ref, own_hbm, obs_hbm, pay_ref, aux_ref, own_ref, obs_ref, sems):
    me = lax.axis_index("y")
    get_own = pltpu.make_async_copy(own_hbm, own_ref, sems.at[0])
    get_obs = pltpu.make_async_copy(obs_hbm, obs_ref, sems.at[1])
    get_own.start()
    get_obs.start()
    get_own.wait()
    x = own_ref[0].astype(F32)
    zx = lanes_sum(x)
    get_obs.wait()
    y = obs_ref[...].astype(F32)
    zy = lanes_sum(y)
    fill_local(scales_ref, x, y, aux_ref)
    row, lane = iota((8, 128), 0), iota((8, 128), 1)

    def high(v):
        return v.astype(BF16).astype(F32)

    part = jnp.zeros((8, 128), F32)
    extra = jnp.zeros((8, 128), F32)
    for k in range(3):
        part = jnp.where(part_of(me, k, lane), zy[:, k * 128 : (k + 1) * 128], part)
        zk = zx[:, k * 128 : (k + 1) * 128]
        extra = jnp.where(row == k, high(zk), extra)
        extra = jnp.where(row == k + 3, zk - high(zk), extra)
    extra = jnp.where(row == 6, high(part), extra)
    extra = jnp.where(row == 7, part - high(part), extra)
    for d in range(GROUP):
        h = d % 2
        pay_ref[d] = jnp.concatenate([x[d // 2, :, h * 128 : (h + 1) * 128], extra], axis=0).astype(BF16)


def distance_kernel(scales_ref, recv_ref, aux_ref, msg_ref, zall_ref, token_ref, rows_ref):
    token_ref[...] = jnp.zeros((8, 128), F32)
    me = lax.axis_index("y")
    inv = inverse_square(scales_ref, me * 2 + lax.axis_index("xl"))
    w = tile_weights((ROWS, 128)) * (inv * np.float32(1.0 / (C * LON * SUMW)))
    row, lane = iota((8, 128), 0), iota((8, 128), 1)
    got = [recv_ref[s].astype(F32) for s in range(GROUP)]
    rows_ref[...] = jnp.zeros((128, 128), F32)
    pairs = [(k, m, (m - k) % M) for k in (1, 2, 3, 4) for m in range(M) if k < 4 or m < 4]

    def put(at, value):
        rows_ref[at : at + 1] = jnp.sum(value, axis=0, keepdims=True)

    totals = [jnp.zeros((8, 128), F32) for _ in pairs]
    for t in range(3):
        rows8 = slice(t * 8, t * 8 + 8)
        for p, (_, m, n) in enumerate(pairs):
            acc = None
            for l in range(4):
                d = got[m * 4 + l][rows8] - got[n * 4 + l][rows8]
                acc = d * d if acc is None else acc + d * d
            totals[p] = totals[p] + acc * w[rows8]
    for p, (k, m, _) in enumerate(pairs):
        put((k - 1) * 8 + m, totals[p])
    rows_ref[32:40] = jnp.where(row == me, jnp.sum(aux_ref[0:8], axis=0, keepdims=True), 0.0)

    zw = aux_ref[8:16]
    real = row < 3
    zobs = jnp.zeros((8, 128), F32)
    zonal = []
    for m in range(M):
        s = sum(got[m * 4 + l][24:32] for l in range(4))
        z = jnp.where(real, s + jnp.concatenate([s[3:8], s[0:3]], axis=0), 0.0) * np.float32(1.0 / LON)
        zonal.append(z)
        zall_ref[m] = z
        part = s[6:7] + s[7:8]
        zobs = jnp.where(real & part_of(m, row, lane), part, zobs)
    zobs = zobs * np.float32(1.0 / LON)
    zall_ref[M] = zobs
    for k, m, n in pairs:
        d = zonal[m] - zonal[n]
        put(40 + (k - 1) * 8 + m, zw * d * d)
    for m in range(M):
        d = zonal[m] - zobs
        put(72 + m, zw * d * d)
    ones = jnp.ones((8, 128), F32)
    sums = lax.dot_general(
        ones, rows_ref[...], (((1,), (1,)), ((), ())), precision=HIGHEST, preferred_element_type=F32
    )
    for i in range(msg_ref.shape[0]):
        msg_ref[i] = sums[0:1]


def relay_kernel(in_ref, out_ref):
    total = jnp.sum(in_ref[...], axis=0)
    out_ref[...] = jnp.broadcast_to(total[None], out_ref.shape)


def stack_kernel(own_ref, up_ref, down_ref, token_ref, ups_ref, downs_ref, again_ref):
    ups_ref[0] = own_ref[0]
    ups_ref[1] = up_ref[...]
    downs_ref[0] = own_ref[0]
    downs_ref[1] = down_ref[...]
    again_ref[...] = up_ref[...]


def coefficient_kernel(msg_ref, zall_ref, coef_ref, zcol_ref):
    me = lax.axis_index("y")
    dist = jnp.sum(msg_ref[...], axis=0)
    row, lane = iota((16, 128), 0), iota((16, 128), 1)
    j = row & 7
    k = j + 1
    at = jnp.where(
        k <= 3,
        j * 8 + ((me + k) & 7),
        jnp.where(k == 4, 24 + (me & 3), jnp.where(k <= 7, (7 - k) * 8 + me, 32 + me)),
    )
    at = at + jnp.where(row >= 8, 40, 0)
    e = jnp.broadcast_to(jnp.exp(dist * np.float32(-0.5 / BAND)), (16, 128))
    picked = jnp.sum(jnp.where(lane == at, e, 0.0), axis=1, keepdims=True)
    norm = jnp.where(j == 7, 1.0 / (M * BAND), 1.0 / (M * (M - 1) * BAND))
    coef = jnp.broadcast_to(picked, (16, 128)) * norm
    coef_ref[...] = coef
    zme = zall_ref[me]
    z = coef[15:16] * (zme - zall_ref[M])
    for k in range(1, M):
        z = z + coef[7 + k : 8 + k] * (zall_ref[(me + k) & 7] - zme)
    for b in range(3):
        zcol_ref[b * 128 : (b + 1) * 128] = jnp.broadcast_to(z[b : b + 1], (128, 128)).T


def mix_kernel(
    scales_ref, coef_ref, zcol_ref, obs_ref, own_ref, t2_ref, t4_ref, t6_ref, ups_ref, downs_ref, out_hbm, out_ref, sems
):
    tiles = [
        own_ref.at[0], ups_ref.at[0], t2_ref, ups_ref.at[1], t4_ref, downs_ref.at[1], t6_ref, downs_ref.at[0]
    ]
    fac = tile_weights((ROWS, COLS)) * np.float32(LAT / SUMW)
    coef = coef_ref[...]
    coef = jnp.concatenate([coef, coef], axis=1)
    per = C // PARTS
    copies = []
    for c in range(C):
        xm = tiles[0][c].astype(F32)
        acc = coef[7:8] * (xm - obs_ref[c].astype(F32))
        for k in range(1, M):
            acc = acc + coef[k - 1 : k] * (tiles[k][c].astype(F32) - xm)
        z = zcol_ref[c * ROWS : (c + 1) * ROWS]
        acc = acc + jnp.concatenate([z, z], axis=1)
        out_ref[c] = acc * (fac * inverse_square(scales_ref, c))
        if c % per == per - 1:
            part = pl.ds(c + 1 - per, per)
            copies.append(pltpu.make_async_copy(out_ref.at[part], out_hbm.at[0, part], sems.at[c // per]))
            copies[-1].start()
    for copy in copies:
        copy.wait()


VMEM = pl.BlockSpec(memory_space=pltpu.VMEM)
SMEM = pl.BlockSpec(memory_space=pltpu.SMEM)


def call(kernel, out_shape, in_specs, cost, vmem=32, **kw):
    return pl.pallas_call(
        kernel,
        out_shape=out_shape,
        in_specs=in_specs,
        cost_estimate=pl.CostEstimate(flops=cost, bytes_accessed=cost, transcendentals=0),
        compiler_params=pltpu.CompilerParams(vmem_limit_bytes=vmem * 1024 * 1024),
        **kw,
    )


def from_ahead(tile, k):
    return lax.ppermute(tile, "y", [((i + k) % M, i) for i in range(M)])


def per_device(members, observed, scales):
    shape = jax.ShapeDtypeStruct
    hbm = pl.BlockSpec(memory_space=pltpu.HBM)
    pay, aux = call(
        pack_kernel,
        (shape((GROUP, 32, 128), BF16), shape((16, 128), F32)),
        [SMEM, hbm, hbm],
        1 << 20,
        vmem=60,
        out_specs=(VMEM, VMEM),
        scratch_shapes=[
            pltpu.VMEM((1, C, ROWS, COLS), BF16),
            pltpu.VMEM((C, ROWS, COLS), BF16),
            pltpu.SemaphoreType.DMA((2,)),
        ],
    )(scales, members, observed)
    tiles = [members[0]] + [None] * 7
    recv = lax.all_to_all(pay, ("y", "xl", "core"), 0, 0, tiled=True)
    tiles[2], tiles[6] = from_ahead(tiles[0], 2), from_ahead(tiles[0], -2)
    msg, zall, token = call(
        distance_kernel,
        (shape((16, 1, 128), F32), shape((16, 8, 128), F32), shape((8, 128), F32)),
        [SMEM, VMEM, VMEM],
        LONG,
        out_specs=(VMEM, VMEM, VMEM),
        scratch_shapes=[pltpu.VMEM((128, 128), F32)],
    )(scales, recv, aux)
    msg = lax.all_to_all(msg, ("xh", "xl", "core"), 0, 0, tiled=True)
    tile = shape((C, ROWS, COLS), BF16)
    pair = shape((2, C, ROWS, COLS), BF16)
    ups, downs, again = call(stack_kernel, (pair, pair, tile), [VMEM] * 4, 1 << 22, out_specs=(VMEM,) * 3)(
        members, tiles[2], tiles[6], token
    )
    ups, downs = from_ahead(ups, 1), from_ahead(downs, -1)
    tiles[4] = from_ahead(again, 2)
    msg = call(relay_kernel, shape((64, 1, 128), F32), [VMEM], LONG, out_specs=VMEM)(msg)
    msg = lax.all_to_all(msg, ("y", "z"), 0, 0, tiled=True)
    coef, zcol = call(
        coefficient_kernel,
        (shape((16, 128), F32), shape((CELLS, 128), F32)),
        [VMEM] * 2,
        1 << 16,
        out_specs=(VMEM, VMEM),
    )(msg, zall)
    return call(
        mix_kernel,
        shape((1, C, ROWS, COLS), F32),
        [SMEM] + [VMEM] * 9,
        1 << 22,
        out_specs=hbm,
        scratch_shapes=[pltpu.VMEM((C, ROWS, COLS), F32), pltpu.SemaphoreType.DMA((PARTS,))],
    )(scales, coef, zcol, observed, members, tiles[2], tiles[4], tiles[6], ups, downs)


def solution(mesh):
    fine = Mesh(mesh.devices.reshape(8, 8, 4, 2, 2), ("y", "z", "xh", "xl", "core"))
    placed = P("y", None, ("z", "xh"), ("xl", "core"))
    return jax.shard_map(
        per_device,
        mesh=fine,
        in_specs=(placed, P(None, ("z", "xh"), ("xl", "core")), P()),
        out_specs=placed,
        check_vma=False,
    )
```

```python
import functools

import jax
import jax.numpy as jnp
import numpy as np
from jax import lax
from jax.experimental import pallas as pl
from jax.experimental.pallas import tpu as pltpu
from jax.sharding import Mesh
from jax.sharding import PartitionSpec as P

BAND = 1.0
F32 = jnp.float32
BF16 = jnp.bfloat16
C, M, LAT, LON = 16, 8, 768, 1024
ROWS, COLS = 24, 256
CELLS = C * ROWS
PIECES = 4
PARTS = 8
GROUP = 32
LONG = 1 << 36
HIGHEST = lax.Precision.HIGHEST


def total_weight():
    index = np.arange(LAT).astype(np.float32)
    angle = (np.float32(-90.0) + (index + np.float32(0.5)) * np.float32(180.0) / np.float32(LAT)) * np.float32(
        np.pi / 180.0
    )
    return float(np.sum(np.cos(angle.astype(np.float32)).astype(np.float64)))


SUMW = total_weight()


def row_weight(index):
    angle = (-90.0 + (index.astype(F32) + 0.5) * 180.0 / LAT) * np.float32(np.pi / 180.0)
    return jnp.cos(angle)


def iota(shape, axis):
    return lax.broadcasted_iota(jnp.int32, shape, axis)


def lat_index():
    return lax.axis_index("z") * 4 + lax.axis_index("xh")


def tile_weights(shape):
    return row_weight(lat_index() * ROWS + iota(shape, 0))


def inverse_square(scales_ref, c):
    s = scales_ref[c]
    return 1.0 / (s * s)


def lanes_sum(x):
    ones = jnp.ones((8, COLS), BF16)
    flat = x.reshape(CELLS, COLS).astype(BF16)
    return lax.dot_general(ones, flat, (((1,), (1,)), ((), ())), preferred_element_type=F32)


def part_of(part, block, lane):
    flat = block * 128 + lane
    return (flat >= part * (CELLS // M)) & (flat < (part + 1) * (CELLS // M))


def pack_kernel(scales_ref, own_hbm, obs_hbm, pay_ref, aux_ref, own_ref, obs_ref, sems):
    me = lax.axis_index("y")
    per = C // PIECES
    copies = []
    for i in range(PIECES):
        part = pl.ds(i * per, per)
        copies.append(
            (
                pltpu.make_async_copy(own_hbm.at[0, part], own_ref.at[part], sems.at[2 * i]),
                pltpu.make_async_copy(obs_hbm.at[part], obs_ref.at[part], sems.at[2 * i + 1]),
            )
        )
        for copy in copies[-1]:
            copy.start()

    w = tile_weights((ROWS, 128))
    flat = iota((8, 128), 0) * 128 + iota((8, 128), 1)
    channel = lax.shift_right_logical(flat * 2731, 16)
    weight = row_weight(lat_index() * ROWS + flat - channel * ROWS)
    inv = jnp.zeros((8, 128), F32)
    for c in range(C):
        inv = jnp.where(channel == c, inverse_square(scales_ref, c), inv)
    aux_ref[8:16] = weight * inv * np.float32(1.0 / (C * SUMW * GROUP))

    total = jnp.zeros((ROWS, 128), F32)
    for i in range(PIECES):
        for copy in copies[i]:
            copy.wait()
        for c in range(i * per, (i + 1) * per):
            x = own_ref[c].astype(F32)
            d = x - obs_ref[c].astype(F32)
            d = d * d
            total = total + (d[:, :128] + d[:, 128:]) * inverse_square(scales_ref, c)
            for h in range(2):
                pay_ref[2 * c + h, 0:16] = x[0:16, h * 128 : (h + 1) * 128].astype(BF16)
    total = total * w
    aux_ref[0:8] = (total[0:8] + total[8:16] + total[16:24]) * np.float32(1.0 / (C * LON * SUMW))

    x = own_ref[...].astype(F32)
    zx = lanes_sum(x)
    zy = lanes_sum(obs_ref[...].astype(F32))
    row, lane = iota((8, 128), 0), iota((8, 128), 1)

    def high(v):
        return v.astype(BF16).astype(F32)

    part = jnp.zeros((8, 128), F32)
    extra = jnp.zeros((8, 128), F32)
    for k in range(3):
        part = jnp.where(part_of(me, k, lane), zy[:, k * 128 : (k + 1) * 128], part)
        zk = zx[:, k * 128 : (k + 1) * 128]
        extra = jnp.where(row == k, high(zk), extra)
        extra = jnp.where(row == k + 3, zk - high(zk), extra)
    extra = jnp.where(row == 6, high(part), extra)
    extra = jnp.where(row == 7, part - high(part), extra)
    for d in range(GROUP):
        h = d % 2
        last = jnp.concatenate([x[d // 2, 16:24, h * 128 : (h + 1) * 128], extra], axis=0)
        pay_ref[d, 16:32] = last.astype(BF16)


def distance_kernel(scales_ref, recv_ref, aux_ref, msg_ref, zall_ref, token_ref, rows_ref):
    token_ref[...] = jnp.zeros((8, 128), F32)
    me = lax.axis_index("y")
    inv = inverse_square(scales_ref, me * 2 + lax.axis_index("xl"))
    w = tile_weights((ROWS, 128)) * (inv * np.float32(1.0 / (C * LON * SUMW)))
    row, lane = iota((8, 128), 0), iota((8, 128), 1)
    got = [recv_ref[s].astype(F32) for s in range(GROUP)]
    rows_ref[...] = jnp.zeros((128, 128), F32)
    pairs = [(k, m, (m - k) % M) for k in (1, 2, 3, 4) for m in range(M) if k < 4 or m < 4]

    def put(at, value):
        rows_ref[at : at + 1] = jnp.sum(value, axis=0, keepdims=True)

    totals = [jnp.zeros((8, 128), F32) for _ in pairs]
    for t in range(3):
        rows8 = slice(t * 8, t * 8 + 8)
        for p, (_, m, n) in enumerate(pairs):
            acc = None
            for l in range(4):
                d = got[m * 4 + l][rows8] - got[n * 4 + l][rows8]
                acc = d * d if acc is None else acc + d * d
            totals[p] = totals[p] + acc * w[rows8]
    for p, (k, m, _) in enumerate(pairs):
        put((k - 1) * 8 + m, totals[p])
    rows_ref[32:40] = jnp.where(row == me, jnp.sum(aux_ref[0:8], axis=0, keepdims=True), 0.0)

    zw = aux_ref[8:16]
    real = row < 3
    zobs = jnp.zeros((8, 128), F32)
    zonal = []
    for m in range(M):
        s = sum(got[m * 4 + l][24:32] for l in range(4))
        z = jnp.where(real, s + jnp.concatenate([s[3:8], s[0:3]], axis=0), 0.0) * np.float32(1.0 / LON)
        zonal.append(z)
        zall_ref[m] = z
        part = s[6:7] + s[7:8]
        zobs = jnp.where(real & part_of(m, row, lane), part, zobs)
    zobs = zobs * np.float32(1.0 / LON)
    zall_ref[M] = zobs
    for k, m, n in pairs:
        d = zonal[m] - zonal[n]
        put(40 + (k - 1) * 8 + m, zw * d * d)
    for m in range(M):
        d = zonal[m] - zobs
        put(72 + m, zw * d * d)
    ones = jnp.ones((8, 128), F32)
    sums = lax.dot_general(
        ones, rows_ref[...], (((1,), (1,)), ((), ())), precision=HIGHEST, preferred_element_type=F32
    )
    for i in range(msg_ref.shape[0]):
        msg_ref[i] = sums[0:1]


def relay_kernel(in_ref, out_ref):
    total = jnp.sum(in_ref[...], axis=0)
    out_ref[...] = jnp.broadcast_to(total[None], out_ref.shape)


def stack_kernel(own_ref, up_ref, down_ref, token_ref, ups_ref, downs_ref):
    half = C // 2
    ups_ref[0:C] = own_ref[0]
    ups_ref[C : 2 * C] = down_ref[...]
    ups_ref[2 * C :] = up_ref[0:half]
    downs_ref[0:C] = own_ref[0]
    downs_ref[C : 2 * C] = up_ref[...]
    downs_ref[2 * C :] = down_ref[half:]


def coefficient_kernel(msg_ref, zall_ref, coef_ref, zcol_ref):
    me = lax.axis_index("y")
    dist = jnp.sum(msg_ref[...], axis=0)
    row, lane = iota((16, 128), 0), iota((16, 128), 1)
    j = row & 7
    k = j + 1
    at = jnp.where(
        k <= 3,
        j * 8 + ((me + k) & 7),
        jnp.where(k == 4, 24 + (me & 3), jnp.where(k <= 7, (7 - k) * 8 + me, 32 + me)),
    )
    at = at + jnp.where(row >= 8, 40, 0)
    e = jnp.broadcast_to(jnp.exp(dist * np.float32(-0.5 / BAND)), (16, 128))
    picked = jnp.sum(jnp.where(lane == at, e, 0.0), axis=1, keepdims=True)
    norm = jnp.where(j == 7, 1.0 / (M * BAND), 1.0 / (M * (M - 1) * BAND))
    coef = jnp.broadcast_to(picked, (16, 128)) * norm
    coef_ref[...] = coef
    zme = zall_ref[me]
    z = coef[15:16] * (zme - zall_ref[M])
    for k in range(1, M):
        z = z + coef[7 + k : 8 + k] * (zall_ref[(me + k) & 7] - zme)
    for b in range(3):
        zcol_ref[b * 128 : (b + 1) * 128] = jnp.broadcast_to(z[b : b + 1], (128, 128)).T


def mix_kernel(
    scales_ref, coef_ref, zcol_ref, obs_ref, own_ref, up_ref, down_ref, ups_ref, downs_ref, out_hbm, out_ref, sems
):
    def tile(k, c):
        if k == 4:
            return ups_ref[2 * C + c] if c < C // 2 else downs_ref[2 * C + c - C // 2]
        return {
            1: ups_ref, 6: ups_ref, 7: downs_ref, 2: downs_ref, 3: up_ref, 5: down_ref
        }[k][c + (C if k in (6, 2) else 0)]

    fac = tile_weights((ROWS, COLS)) * np.float32(LAT / SUMW)
    coef = coef_ref[...]
    coef = jnp.concatenate([coef, coef], axis=1)
    per = C // PARTS
    copies = []
    for c in range(C):
        xm = own_ref[0, c].astype(F32)
        acc = coef[7:8] * (xm - obs_ref[c].astype(F32))
        for k in range(1, M):
            acc = acc + coef[k - 1 : k] * (tile(k, c).astype(F32) - xm)
        z = zcol_ref[c * ROWS : (c + 1) * ROWS]
        acc = acc + jnp.concatenate([z, z], axis=1)
        out_ref[c] = acc * (fac * inverse_square(scales_ref, c))
        if c % per == per - 1:
            part = pl.ds(c + 1 - per, per)
            copies.append(pltpu.make_async_copy(out_ref.at[part], out_hbm.at[0, part], sems.at[c // per]))
            copies[-1].start()
    for copy in copies:
        copy.wait()


VMEM = pl.BlockSpec(memory_space=pltpu.VMEM)
SMEM = pl.BlockSpec(memory_space=pltpu.SMEM)


def call(kernel, out_shape, in_specs, cost, vmem=32, **kw):
    return pl.pallas_call(
        kernel,
        out_shape=out_shape,
        in_specs=in_specs,
        cost_estimate=pl.CostEstimate(flops=cost, bytes_accessed=cost, transcendentals=0),
        compiler_params=pltpu.CompilerParams(vmem_limit_bytes=vmem * 1024 * 1024),
        **kw,
    )


def from_ahead(tile, k):
    return lax.ppermute(tile, "y", [((i + k) % M, i) for i in range(M)])


def per_device(members, observed, scales):
    shape = jax.ShapeDtypeStruct
    hbm = pl.BlockSpec(memory_space=pltpu.HBM)
    pay, aux = call(
        pack_kernel,
        (shape((GROUP, 32, 128), BF16), shape((16, 128), F32)),
        [SMEM, hbm, hbm],
        1 << 20,
        vmem=60,
        out_specs=(VMEM, VMEM),
        scratch_shapes=[
            pltpu.VMEM((C, ROWS, COLS), BF16),
            pltpu.VMEM((C, ROWS, COLS), BF16),
            pltpu.SemaphoreType.DMA((2 * PIECES,)),
        ],
    )(scales, members, observed)
    recv = lax.all_to_all(pay, ("y", "xl", "core"), 0, 0, tiled=True)
    up, down = from_ahead(members[0], 3), from_ahead(members[0], -3)
    msg, zall, token = call(
        distance_kernel,
        (shape((16, 1, 128), F32), shape((16, 8, 128), F32), shape((8, 128), F32)),
        [SMEM, VMEM, VMEM],
        LONG,
        out_specs=(VMEM, VMEM, VMEM),
        scratch_shapes=[pltpu.VMEM((128, 128), F32)],
    )(scales, recv, aux)
    msg = lax.all_to_all(msg, ("xh", "xl", "core"), 0, 0, tiled=True)
    stack = shape((5 * C // 2, ROWS, COLS), BF16)
    ups, downs = call(stack_kernel, (stack, stack), [VMEM] * 4, 1 << 22, out_specs=(VMEM,) * 2)(
        members, up, down, token
    )
    ups, downs = from_ahead(ups, 1), from_ahead(downs, -1)
    msg = call(relay_kernel, shape((64, 1, 128), F32), [VMEM], LONG, out_specs=VMEM)(msg)
    msg = lax.all_to_all(msg, ("y", "z"), 0, 0, tiled=True)
    coef, zcol = call(
        coefficient_kernel,
        (shape((16, 128), F32), shape((CELLS, 128), F32)),
        [VMEM] * 2,
        1 << 16,
        out_specs=(VMEM, VMEM),
    )(msg, zall)
    return call(
        mix_kernel,
        shape((1, C, ROWS, COLS), F32),
        [SMEM] + [VMEM] * 8,
        1 << 22,
        out_specs=hbm,
        scratch_shapes=[pltpu.VMEM((C, ROWS, COLS), F32), pltpu.SemaphoreType.DMA((PARTS,))],
    )(scales, coef, zcol, observed, members, up, down, ups, downs)


def solution(mesh):
    fine = Mesh(mesh.devices.reshape(8, 8, 4, 2, 2), ("y", "z", "xh", "xl", "core"))
    placed = P("y", None, ("z", "xh"), ("xl", "core"))
    return jax.shard_map(
        per_device,
        mesh=fine,
        in_specs=(placed, P(None, ("z", "xh"), ("xl", "core")), P()),
        out_specs=placed,
        check_vma=False,
    )
```

```python
import functools

import jax
import jax.numpy as jnp
import numpy as np
from jax import lax
from jax.experimental import pallas as pl
from jax.experimental.pallas import tpu as pltpu
from jax.sharding import Mesh
from jax.sharding import PartitionSpec as P

BAND = 1.0
F32 = jnp.float32
BF16 = jnp.bfloat16
C, M, LAT, LON = 16, 8, 768, 1024
ROWS, COLS = 24, 256
CELLS = C * ROWS
PIECES = 4
PARTS = 8
GROUP = 32
LONG = 1 << 36
HIGHEST = lax.Precision.HIGHEST


def total_weight():
    index = np.arange(LAT).astype(np.float32)
    angle = (np.float32(-90.0) + (index + np.float32(0.5)) * np.float32(180.0) / np.float32(LAT)) * np.float32(
        np.pi / 180.0
    )
    return float(np.sum(np.cos(angle.astype(np.float32)).astype(np.float64)))


SUMW = total_weight()


def row_weight(index):
    angle = (-90.0 + (index.astype(F32) + 0.5) * 180.0 / LAT) * np.float32(np.pi / 180.0)
    return jnp.cos(angle)


def iota(shape, axis):
    return lax.broadcasted_iota(jnp.int32, shape, axis)


def lat_index():
    return lax.axis_index("z") * 4 + lax.axis_index("xh")


def tile_weights(shape):
    return row_weight(lat_index() * ROWS + iota(shape, 0))


def inverse_square(scales_ref, c, rows=8):
    s = jnp.full((8, 128), scales_ref[c], F32)
    return jnp.concatenate([1.0 / (s * s)] * (rows // 8), axis=0)


def lanes_sum(x):
    ones = jnp.ones((8, COLS), BF16)
    flat = x.reshape(CELLS, COLS).astype(BF16)
    return lax.dot_general(ones, flat, (((1,), (1,)), ((), ())), preferred_element_type=F32)


def part_of(part, block, lane):
    flat = block * 128 + lane
    return (flat >= part * (CELLS // M)) & (flat < (part + 1) * (CELLS // M))


def pack_kernel(scales_ref, own_hbm, obs_hbm, pay_ref, aux_ref, own_ref, obs_ref, sems):
    me = lax.axis_index("y")
    per = C // PIECES
    copies = []
    for i in range(PIECES):
        part = pl.ds(i * per, per)
        copies.append(
            (
                pltpu.make_async_copy(own_hbm.at[0, part], own_ref.at[part], sems.at[2 * i]),
                pltpu.make_async_copy(obs_hbm.at[part], obs_ref.at[part], sems.at[2 * i + 1]),
            )
        )
        for copy in copies[-1]:
            copy.start()

    w = tile_weights((ROWS, 128))
    flat = iota((8, 128), 0) * 128 + iota((8, 128), 1)
    channel = lax.shift_right_logical(flat * 2731, 16)
    weight = row_weight(lat_index() * ROWS + flat - channel * ROWS)
    inv = jnp.zeros((8, 128), F32)
    for c in range(C):
        inv = jnp.where(channel == c, inverse_square(scales_ref, c), inv)
    aux_ref[8:16] = weight * inv * np.float32(1.0 / (C * SUMW * GROUP))

    total = jnp.zeros((ROWS, 128), F32)
    for i in range(PIECES):
        for copy in copies[i]:
            copy.wait()
        for c in range(i * per, (i + 1) * per):
            x = own_ref[c].astype(F32)
            d = x - obs_ref[c].astype(F32)
            d = d * d
            total = total + (d[:, :128] + d[:, 128:]) * inverse_square(scales_ref, c, ROWS)
            for h in range(2):
                pay_ref[2 * c + h, 0:16] = x[0:16, h * 128 : (h + 1) * 128].astype(BF16)
    total = total * w
    aux_ref[0:8] = (total[0:8] + total[8:16] + total[16:24]) * np.float32(1.0 / (C * LON * SUMW))

    x = own_ref[...].astype(F32)
    zx = lanes_sum(x)
    zy = lanes_sum(obs_ref[...].astype(F32))
    row, lane = iota((8, 128), 0), iota((8, 128), 1)

    def high(v):
        return v.astype(BF16).astype(F32)

    part = jnp.zeros((8, 128), F32)
    extra = jnp.zeros((8, 128), F32)
    for k in range(3):
        part = jnp.where(part_of(me, k, lane), zy[:, k * 128 : (k + 1) * 128], part)
        zk = zx[:, k * 128 : (k + 1) * 128]
        extra = jnp.where(row == k, high(zk), extra)
        extra = jnp.where(row == k + 3, zk - high(zk), extra)
    extra = jnp.where(row == 6, high(part), extra)
    extra = jnp.where(row == 7, part - high(part), extra)
    for d in range(GROUP):
        h = d % 2
        last = jnp.concatenate([x[d // 2, 16:24, h * 128 : (h + 1) * 128], extra], axis=0)
        pay_ref[d, 16:32] = last.astype(BF16)


def distance_kernel(scales_ref, recv_ref, aux_ref, msg_ref, zall_ref, token_ref, rows_ref):
    token_ref[...] = jnp.zeros((8, 128), F32)
    me = lax.axis_index("y")
    inv = inverse_square(scales_ref, me * 2 + lax.axis_index("xl"), ROWS)
    w = tile_weights((ROWS, 128)) * (inv * np.float32(1.0 / (C * LON * SUMW)))
    row, lane = iota((8, 128), 0), iota((8, 128), 1)
    got = [recv_ref[s].astype(F32) for s in range(GROUP)]
    rows_ref[...] = jnp.zeros((128, 128), F32)
    pairs = [(k, m, (m - k) % M) for k in (1, 2, 3, 4) for m in range(M) if k < 4 or m < 4]

    def put(at, value):
        rows_ref[at : at + 1] = jnp.sum(value, axis=0, keepdims=True)

    totals = [jnp.zeros((8, 128), F32) for _ in pairs]
    for t in range(3):
        rows8 = slice(t * 8, t * 8 + 8)
        for p, (_, m, n) in enumerate(pairs):
            acc = None
            for l in range(4):
                d = got[m * 4 + l][rows8] - got[n * 4 + l][rows8]
                acc = d * d if acc is None else acc + d * d
            totals[p] = totals[p] + acc * w[rows8]
    for p, (k, m, _) in enumerate(pairs):
        put((k - 1) * 8 + m, totals[p])
    rows_ref[32:40] = jnp.where(row == me, jnp.sum(aux_ref[0:8], axis=0, keepdims=True), 0.0)

    zw = aux_ref[8:16]
    real = row < 3
    zobs = jnp.zeros((8, 128), F32)
    zonal = []
    for m in range(M):
        s = sum(got[m * 4 + l][24:32] for l in range(4))
        z = jnp.where(real, s + jnp.concatenate([s[3:8], s[0:3]], axis=0), 0.0) * np.float32(1.0 / LON)
        zonal.append(z)
        zall_ref[m] = z
        part = s[6:7] + s[7:8]
        zobs = jnp.where(real & part_of(m, row, lane), part, zobs)
    zobs = zobs * np.float32(1.0 / LON)
    zall_ref[M] = zobs
    for k, m, n in pairs:
        d = zonal[m] - zonal[n]
        put(40 + (k - 1) * 8 + m, zw * d * d)
    for m in range(M):
        d = zonal[m] - zobs
        put(72 + m, zw * d * d)
    ones = jnp.ones((8, 128), F32)
    sums = lax.dot_general(
        ones, rows_ref[...], (((1,), (1,)), ((), ())), precision=HIGHEST, preferred_element_type=F32
    )
    for i in range(msg_ref.shape[0]):
        msg_ref[i] = sums[0:1]


def relay_kernel(in_ref, out_ref):
    total = jnp.sum(in_ref[...], axis=0)
    out_ref[...] = jnp.broadcast_to(total[None], out_ref.shape)


def stack_kernel(own_ref, up_ref, down_ref, token_ref, ups_ref, downs_ref):
    half = C // 2
    ups_ref[0:C] = own_ref[0]
    ups_ref[C : 2 * C] = down_ref[...]
    ups_ref[2 * C :] = up_ref[0:half]
    downs_ref[0:C] = own_ref[0]
    downs_ref[C : 2 * C] = up_ref[...]
    downs_ref[2 * C :] = down_ref[half:]


def coefficient_kernel(msg_ref, zall_ref, coef_ref, zcol_ref):
    me = lax.axis_index("y")
    dist = jnp.sum(msg_ref[...], axis=0)
    row, lane = iota((16, 128), 0), iota((16, 128), 1)
    j = row & 7
    k = j + 1
    at = jnp.where(
        k <= 3,
        j * 8 + ((me + k) & 7),
        jnp.where(k == 4, 24 + (me & 3), jnp.where(k <= 7, (7 - k) * 8 + me, 32 + me)),
    )
    at = at + jnp.where(row >= 8, 40, 0)
    e = jnp.broadcast_to(jnp.exp(dist * np.float32(-0.5 / BAND)), (16, 128))
    picked = jnp.sum(jnp.where(lane == at, e, 0.0), axis=1, keepdims=True)
    norm = jnp.where(j == 7, 1.0 / (M * BAND), 1.0 / (M * (M - 1) * BAND))
    coef = jnp.broadcast_to(picked, (16, 128)) * norm
    coef_ref[...] = coef
    zme = zall_ref[me]
    z = coef[15:16] * (zme - zall_ref[M])
    for k in range(1, M):
        z = z + coef[7 + k : 8 + k] * (zall_ref[(me + k) & 7] - zme)
    for b in range(3):
        zcol_ref[b * 128 : (b + 1) * 128] = jnp.broadcast_to(z[b : b + 1], (128, 128)).T


def mix_kernel(
    scales_ref, coef_ref, zcol_ref, obs_ref, own_ref, up_ref, down_ref, ups_ref, downs_ref, out_hbm, out_ref, sems
):
    def tile(k, c):
        if k == 4:
            return ups_ref[2 * C + c] if c < C // 2 else downs_ref[2 * C + c - C // 2]
        return {
            1: ups_ref, 6: ups_ref, 7: downs_ref, 2: downs_ref, 3: up_ref, 5: down_ref
        }[k][c + (C if k in (6, 2) else 0)]

    fac = tile_weights((ROWS, 128)) * np.float32(LAT / SUMW)
    coef = coef_ref[...]
    coef = jnp.concatenate([coef, coef], axis=1)
    per = C // PARTS
    copies = []
    for c in range(C):
        xm = own_ref[0, c].astype(F32)
        acc = coef[7:8] * (xm - obs_ref[c].astype(F32))
        for k in range(1, M):
            acc = acc + coef[k - 1 : k] * (tile(k, c).astype(F32) - xm)
        z = zcol_ref[c * ROWS : (c + 1) * ROWS]
        acc = acc + jnp.concatenate([z, z], axis=1)
        f = fac * inverse_square(scales_ref, c, ROWS)
        out_ref[c] = acc * jnp.concatenate([f, f], axis=1)
        if c % per == per - 1:
            part = pl.ds(c + 1 - per, per)
            copies.append(pltpu.make_async_copy(out_ref.at[part], out_hbm.at[0, part], sems.at[c // per]))
            copies[-1].start()
    for copy in copies:
        copy.wait()


VMEM = pl.BlockSpec(memory_space=pltpu.VMEM)
SMEM = pl.BlockSpec(memory_space=pltpu.SMEM)


def call(kernel, out_shape, in_specs, cost, vmem=32, **kw):
    return pl.pallas_call(
        kernel,
        out_shape=out_shape,
        in_specs=in_specs,
        cost_estimate=pl.CostEstimate(flops=cost, bytes_accessed=cost, transcendentals=0),
        compiler_params=pltpu.CompilerParams(vmem_limit_bytes=vmem * 1024 * 1024),
        **kw,
    )


def from_ahead(tile, k):
    return lax.ppermute(tile, "y", [((i + k) % M, i) for i in range(M)])


def per_device(members, observed, scales):
    shape = jax.ShapeDtypeStruct
    hbm = pl.BlockSpec(memory_space=pltpu.HBM)
    pay, aux = call(
        pack_kernel,
        (shape((GROUP, 32, 128), BF16), shape((16, 128), F32)),
        [SMEM, hbm, hbm],
        1 << 20,
        vmem=60,
        out_specs=(VMEM, VMEM),
        scratch_shapes=[
            pltpu.VMEM((C, ROWS, COLS), BF16),
            pltpu.VMEM((C, ROWS, COLS), BF16),
            pltpu.SemaphoreType.DMA((2 * PIECES,)),
        ],
    )(scales, members, observed)
    recv = lax.all_to_all(pay, ("y", "xl", "core"), 0, 0, tiled=True)
    up, down = from_ahead(members[0], 3), from_ahead(members[0], -3)
    msg, zall, token = call(
        distance_kernel,
        (shape((64, 1, 128), F32), shape((16, 8, 128), F32), shape((8, 128), F32)),
        [SMEM, VMEM, VMEM],
        LONG,
        out_specs=(VMEM, VMEM, VMEM),
        scratch_shapes=[pltpu.VMEM((128, 128), F32)],
    )(scales, recv, aux)
    msg = lax.all_to_all(msg, ("y", "z"), 0, 0, tiled=True)
    stack = shape((5 * C // 2, ROWS, COLS), BF16)
    ups, downs = call(stack_kernel, (stack, stack), [VMEM] * 4, 1 << 22, out_specs=(VMEM,) * 2)(
        members, up, down, token
    )
    ups, downs = from_ahead(ups, 1), from_ahead(downs, -1)
    msg = call(relay_kernel, shape((16, 1, 128), F32), [VMEM], LONG, out_specs=VMEM)(msg)
    msg = lax.all_to_all(msg, ("xh", "xl", "core"), 0, 0, tiled=True)
    coef, zcol = call(
        coefficient_kernel,
        (shape((16, 128), F32), shape((CELLS, 128), F32)),
        [VMEM] * 2,
        1 << 16,
        out_specs=(VMEM, VMEM),
    )(msg, zall)
    return call(
        mix_kernel,
        shape((1, C, ROWS, COLS), F32),
        [SMEM] + [VMEM] * 8,
        1 << 22,
        out_specs=hbm,
        scratch_shapes=[pltpu.VMEM((C, ROWS, COLS), F32), pltpu.SemaphoreType.DMA((PARTS,))],
    )(scales, coef, zcol, observed, members, up, down, ups, downs)


def solution(mesh):
    fine = Mesh(mesh.devices.reshape(8, 8, 4, 2, 2), ("y", "z", "xh", "xl", "core"))
    placed = P("y", None, ("z", "xh"), ("xl", "core"))
    return jax.shard_map(
        per_device,
        mesh=fine,
        in_specs=(placed, P(None, ("z", "xh"), ("xl", "core")), P()),
        out_specs=placed,
        check_vma=False,
    )
```

```python
import functools

import jax
import jax.numpy as jnp
import numpy as np
from jax import lax
from jax.experimental import pallas as pl
from jax.experimental.pallas import tpu as pltpu
from jax.sharding import Mesh
from jax.sharding import PartitionSpec as P

BAND = 1.0
F32 = jnp.float32
BF16 = jnp.bfloat16
C, M, LAT, LON = 16, 8, 768, 1024
ROWS, COLS = 24, 256
CELLS = C * ROWS
FIRST = 8
INV = 16
PIECES = 4
PARTS = 8
GROUP = 32
LONG = 1 << 36
HIGHEST = lax.Precision.HIGHEST


def total_weight():
    index = np.arange(LAT).astype(np.float32)
    angle = (np.float32(-90.0) + (index + np.float32(0.5)) * np.float32(180.0) / np.float32(LAT)) * np.float32(
        np.pi / 180.0
    )
    return float(np.sum(np.cos(angle.astype(np.float32)).astype(np.float64)))


SUMW = total_weight()


def row_weight(index):
    angle = (-90.0 + (index.astype(F32) + 0.5) * 180.0 / LAT) * np.float32(np.pi / 180.0)
    return jnp.cos(angle)


def iota(shape, axis):
    return lax.broadcasted_iota(jnp.int32, shape, axis)


def lat_index():
    return lax.axis_index("z") * 4 + lax.axis_index("xh")


def tile_weights(shape):
    return row_weight(lat_index() * ROWS + iota(shape, 0))


def inverse_square(scales_ref, c, rows=8):
    s = jnp.full((8, 128), scales_ref[c], F32)
    return jnp.concatenate([1.0 / (s * s)] * (rows // 8), axis=0)


def lanes_sum(x):
    ones = jnp.ones((8, COLS), BF16)
    flat = x.reshape(CELLS, COLS).astype(BF16)
    return lax.dot_general(ones, flat, (((1,), (1,)), ((), ())), preferred_element_type=F32)


def part_of(part, block, lane):
    flat = block * 128 + lane
    return (flat >= part * (CELLS // M)) & (flat < (part + 1) * (CELLS // M))


def pack_kernel(scales_hbm, own_hbm, obs_hbm, pay_ref, aux_ref, scales_ref, own_ref, obs_ref, sems):
    me = lax.axis_index("y")
    per = C // PIECES
    get_scales = pltpu.make_async_copy(scales_hbm, scales_ref, sems.at[2 * PIECES])
    get_scales.start()
    copies = []
    for i in range(PIECES):
        part = pl.ds(i * per, per)
        copies.append(
            (
                pltpu.make_async_copy(own_hbm.at[0, part], own_ref.at[part], sems.at[2 * i]),
                pltpu.make_async_copy(obs_hbm.at[part], obs_ref.at[part], sems.at[2 * i + 1]),
            )
        )
        for copy in copies[-1]:
            copy.start()

    w = tile_weights((ROWS, 128))
    flat = iota((8, 128), 0) * 128 + iota((8, 128), 1)
    channel = lax.shift_right_logical(flat * 2731, 16)
    weight = row_weight(lat_index() * ROWS + flat - channel * ROWS)
    inv = jnp.zeros((8, 128), F32)
    get_scales.wait()
    for c in range(C):
        one = inverse_square(scales_ref, c)
        aux_ref[INV + c : INV + c + 1] = one[0:1]
        inv = jnp.where(channel == c, one, inv)
    aux_ref[8:16] = weight * inv * np.float32(1.0 / (C * SUMW * GROUP))

    total = jnp.zeros((ROWS, 128), F32)
    for i in range(PIECES):
        for copy in copies[i]:
            copy.wait()
        for c in range(i * per, (i + 1) * per):
            x = own_ref[c].astype(F32)
            d = x - obs_ref[c].astype(F32)
            d = d * d
            total = total + (d[:, :128] + d[:, 128:]) * inverse_square(scales_ref, c, ROWS)
            for h in range(2):
                pay_ref[2 * c + h, 0:16] = x[0:16, h * 128 : (h + 1) * 128].astype(BF16)
    total = total * w
    aux_ref[0:8] = (total[0:8] + total[8:16] + total[16:24]) * np.float32(1.0 / (C * LON * SUMW))

    x = own_ref[...].astype(F32)
    zx = lanes_sum(x)
    zy = lanes_sum(obs_ref[...].astype(F32))
    row, lane = iota((8, 128), 0), iota((8, 128), 1)

    def high(v):
        return v.astype(BF16).astype(F32)

    part = jnp.zeros((8, 128), F32)
    extra = jnp.zeros((8, 128), F32)
    for k in range(3):
        part = jnp.where(part_of(me, k, lane), zy[:, k * 128 : (k + 1) * 128], part)
        zk = zx[:, k * 128 : (k + 1) * 128]
        extra = jnp.where(row == k, high(zk), extra)
        extra = jnp.where(row == k + 3, zk - high(zk), extra)
    extra = jnp.where(row == 6, high(part), extra)
    extra = jnp.where(row == 7, part - high(part), extra)
    for d in range(GROUP):
        h = d % 2
        last = jnp.concatenate([x[d // 2, 16:24, h * 128 : (h + 1) * 128], extra], axis=0)
        pay_ref[d, 16:32] = last.astype(BF16)


def distance_kernel(recv_ref, aux_ref, msg_ref, zall_ref, token_ref, rows_ref):
    token_ref[...] = jnp.zeros((8, 128), F32)
    me = lax.axis_index("y")
    inv = aux_ref[pl.ds(INV + me * 2 + lax.axis_index("xl"), 1)]
    w = tile_weights((ROWS, 128)) * (inv * np.float32(1.0 / (C * LON * SUMW)))
    row, lane = iota((8, 128), 0), iota((8, 128), 1)
    got = [recv_ref[s].astype(F32) for s in range(GROUP)]
    rows_ref[...] = jnp.zeros((128, 128), F32)
    pairs = [(k, m, (m - k) % M) for k in (1, 2, 3, 4) for m in range(M) if k < 4 or m < 4]

    def put(at, value):
        rows_ref[at : at + 1] = jnp.sum(value, axis=0, keepdims=True)

    totals = [jnp.zeros((8, 128), F32) for _ in pairs]
    for t in range(3):
        rows8 = slice(t * 8, t * 8 + 8)
        for p, (_, m, n) in enumerate(pairs):
            acc = None
            for l in range(4):
                d = got[m * 4 + l][rows8] - got[n * 4 + l][rows8]
                acc = d * d if acc is None else acc + d * d
            totals[p] = totals[p] + acc * w[rows8]
    for p, (k, m, _) in enumerate(pairs):
        put((k - 1) * 8 + m, totals[p])
    rows_ref[32:40] = jnp.where(row == me, jnp.sum(aux_ref[0:8], axis=0, keepdims=True), 0.0)

    zw = aux_ref[8:16]
    real = row < 3
    zobs = jnp.zeros((8, 128), F32)
    zonal = []
    for m in range(M):
        s = sum(got[m * 4 + l][24:32] for l in range(4))
        z = jnp.where(real, s + jnp.concatenate([s[3:8], s[0:3]], axis=0), 0.0) * np.float32(1.0 / LON)
        zonal.append(z)
        zall_ref[m] = z
        part = s[6:7] + s[7:8]
        zobs = jnp.where(real & part_of(m, row, lane), part, zobs)
    zobs = zobs * np.float32(1.0 / LON)
    zall_ref[M] = zobs
    for k, m, n in pairs:
        d = zonal[m] - zonal[n]
        put(40 + (k - 1) * 8 + m, zw * d * d)
    for m in range(M):
        d = zonal[m] - zobs
        put(72 + m, zw * d * d)
    ones = jnp.ones((8, 128), F32)
    sums = lax.dot_general(
        ones, rows_ref[...], (((1,), (1,)), ((), ())), precision=HIGHEST, preferred_element_type=F32
    )
    for i in range(msg_ref.shape[0]):
        msg_ref[i] = sums[0:1]


def relay_kernel(in_ref, out_ref):
    total = jnp.sum(in_ref[...], axis=0)
    out_ref[...] = jnp.broadcast_to(total[None], out_ref.shape)


def stack_kernel(own_ref, up_ref, down_ref, token_ref, ups_ref, downs_ref):
    ups_ref[0:C] = up_ref[...]
    ups_ref[C : 2 * C] = down_ref[...]
    ups_ref[2 * C :] = own_ref[0, 0:FIRST]
    downs_ref[0:C] = own_ref[0]
    downs_ref[C : 2 * C] = down_ref[...]
    downs_ref[2 * C :] = up_ref[FIRST:]


def coefficient_kernel(msg_ref, zall_ref, obs_ref, own_ref, up_ref, down_ref, coef_ref, begun_ref, zcol_ref):
    me = lax.axis_index("y")
    dist = jnp.sum(msg_ref[...], axis=0)
    row, lane = iota((16, 128), 0), iota((16, 128), 1)
    j = row & 7
    k = j + 1
    at = jnp.where(
        k <= 3,
        j * 8 + ((me + k) & 7),
        jnp.where(k == 4, 24 + (me & 3), jnp.where(k <= 7, (7 - k) * 8 + me, 32 + me)),
    )
    at = at + jnp.where(row >= 8, 40, 0)
    e = jnp.broadcast_to(jnp.exp(dist * np.float32(-0.5 / BAND)), (16, 128))
    picked = jnp.sum(jnp.where(lane == at, e, 0.0), axis=1, keepdims=True)
    norm = jnp.where(j == 7, 1.0 / (M * BAND), 1.0 / (M * (M - 1) * BAND))
    coef = jnp.broadcast_to(picked, (16, 128)) * norm
    coef_ref[...] = coef
    zme = zall_ref[me]
    z = coef[15:16] * (zme - zall_ref[M])
    for k in range(1, M):
        z = z + coef[7 + k : 8 + k] * (zall_ref[(me + k) & 7] - zme)
    for b in range(3):
        zcol_ref[b * 128 : (b + 1) * 128] = jnp.broadcast_to(z[b : b + 1], (128, 128)).T
    coef = jnp.concatenate([coef, coef], axis=1)
    for c in range(C):
        xm = own_ref[0, c].astype(F32)
        acc = coef[7:8] * (xm - obs_ref[c].astype(F32))
        acc = acc + coef[1:2] * (up_ref[c].astype(F32) - xm)
        acc = acc + coef[4:5] * (down_ref[c].astype(F32) - xm)
        z = zcol_ref[c * ROWS : (c + 1) * ROWS]
        begun_ref[c] = acc + jnp.concatenate([z, z], axis=1)


def mix_kernel(aux_ref, coef_ref, begun_ref, own_ref, ups_ref, downs_ref, out_hbm, out_ref, sems):
    def tile(k, c):
        if k == 1:
            return ups_ref[2 * C + c] if c < FIRST else downs_ref[2 * C + c - FIRST]
        return {3: ups_ref, 6: ups_ref, 7: downs_ref, 4: downs_ref}[k][c + (C if k in (6, 4) else 0)]

    fac = tile_weights((ROWS, 128)) * np.float32(LAT / SUMW)
    coef = coef_ref[...]
    coef = jnp.concatenate([coef, coef], axis=1)
    per = C // PARTS
    copies = []
    for c in range(C):
        xm = own_ref[0, c].astype(F32)
        acc = begun_ref[c]
        for k in (1, 3, 4, 6, 7):
            acc = acc + coef[k - 1 : k] * (tile(k, c).astype(F32) - xm)
        f = fac * aux_ref[INV + c : INV + c + 1]
        out_ref[c] = acc * jnp.concatenate([f, f], axis=1)
        if c % per == per - 1:
            part = pl.ds(c + 1 - per, per)
            copies.append(pltpu.make_async_copy(out_ref.at[part], out_hbm.at[0, part], sems.at[c // per]))
            copies[-1].start()
    for copy in copies:
        copy.wait()


VMEM = pl.BlockSpec(memory_space=pltpu.VMEM)
SMEM = pl.BlockSpec(memory_space=pltpu.SMEM)


def call(kernel, out_shape, in_specs, cost, vmem=32, **kw):
    return pl.pallas_call(
        kernel,
        out_shape=out_shape,
        in_specs=in_specs,
        cost_estimate=pl.CostEstimate(flops=cost, bytes_accessed=cost, transcendentals=0),
        compiler_params=pltpu.CompilerParams(vmem_limit_bytes=vmem * 1024 * 1024),
        **kw,
    )


def from_ahead(tile, k):
    return lax.ppermute(tile, "y", [((i + k) % M, i) for i in range(M)])


def per_device(members, observed, scales):
    shape = jax.ShapeDtypeStruct
    hbm = pl.BlockSpec(memory_space=pltpu.HBM)
    pay, aux = call(
        pack_kernel,
        (shape((GROUP, 32, 128), BF16), shape((INV + C, 128), F32)),
        [hbm] * 3,
        1 << 20,
        vmem=60,
        out_specs=(VMEM, VMEM),
        scratch_shapes=[
            pltpu.SMEM((C,), F32),
            pltpu.VMEM((C, ROWS, COLS), BF16),
            pltpu.VMEM((C, ROWS, COLS), BF16),
            pltpu.SemaphoreType.DMA((2 * PIECES + 1,)),
        ],
    )(scales, members, observed)
    recv = lax.all_to_all(pay, ("y", "xl", "core"), 0, 0, tiled=True)
    up, down = from_ahead(members[0], 2), from_ahead(members[0], -3)
    msg, zall, token = call(
        distance_kernel,
        (shape((64, 1, 128), F32), shape((16, 8, 128), F32), shape((8, 128), F32)),
        [VMEM, VMEM],
        LONG,
        out_specs=(VMEM, VMEM, VMEM),
        scratch_shapes=[pltpu.VMEM((128, 128), F32)],
    )(recv, aux)
    msg = lax.all_to_all(msg, ("y", "z"), 0, 0, tiled=True)
    stacks = tuple(shape((2 * C + n, ROWS, COLS), BF16) for n in (FIRST, C - FIRST))
    ups, downs = call(stack_kernel, stacks, [VMEM] * 4, 1 << 22, out_specs=(VMEM,) * 2)(
        members, up, down, token
    )
    ups, downs = from_ahead(ups, 1), from_ahead(downs, -1)
    msg = call(relay_kernel, shape((16, 1, 128), F32), [VMEM], LONG, out_specs=VMEM)(msg)
    msg = lax.all_to_all(msg, ("xh", "xl", "core"), 0, 0, tiled=True)
    coef, begun = call(
        coefficient_kernel,
        (shape((16, 128), F32), shape((C, ROWS, COLS), F32)),
        [VMEM] * 6,
        1 << 16,
        out_specs=(VMEM, VMEM),
        scratch_shapes=[pltpu.VMEM((CELLS, 128), F32)],
    )(msg, zall, observed, members, up, down)
    return call(
        mix_kernel,
        shape((1, C, ROWS, COLS), F32),
        [VMEM] * 6,
        1 << 22,
        out_specs=hbm,
        scratch_shapes=[pltpu.VMEM((C, ROWS, COLS), F32), pltpu.SemaphoreType.DMA((PARTS,))],
    )(aux, coef, begun, members, ups, downs)


def solution(mesh):
    fine = Mesh(mesh.devices.reshape(8, 8, 4, 2, 2), ("y", "z", "xh", "xl", "core"))
    placed = P("y", None, ("z", "xh"), ("xl", "core"))
    return jax.shard_map(
        per_device,
        mesh=fine,
        in_specs=(placed, P(None, ("z", "xh"), ("xl", "core")), P()),
        out_specs=placed,
        check_vma=False,
    )
```

```python
import functools

import jax
import jax.numpy as jnp
import numpy as np
from jax import lax
from jax.experimental import pallas as pl
from jax.experimental.pallas import tpu as pltpu
from jax.sharding import Mesh
from jax.sharding import PartitionSpec as P

BAND = 1.0
F32 = jnp.float32
BF16 = jnp.bfloat16
C, M, LAT, LON = 16, 8, 768, 1024
ROWS, COLS = 24, 256
CELLS = C * ROWS
FIRST = 8
INV = 16
PIECES = 4
PARTS = 8
GROUP = 32
LONG = 1 << 36
HIGHEST = lax.Precision.HIGHEST


def total_weight():
    index = np.arange(LAT).astype(np.float32)
    angle = (np.float32(-90.0) + (index + np.float32(0.5)) * np.float32(180.0) / np.float32(LAT)) * np.float32(
        np.pi / 180.0
    )
    return float(np.sum(np.cos(angle.astype(np.float32)).astype(np.float64)))


SUMW = total_weight()


def row_weight(index):
    angle = (-90.0 + (index.astype(F32) + 0.5) * 180.0 / LAT) * np.float32(np.pi / 180.0)
    return jnp.cos(angle)


def iota(shape, axis):
    return lax.broadcasted_iota(jnp.int32, shape, axis)


def lat_index():
    return lax.axis_index("z") * 4 + lax.axis_index("xh")


def tile_weights(shape):
    return row_weight(lat_index() * ROWS + iota(shape, 0))


def inverse_square(scales_ref, c, rows=8):
    s = jnp.full((8, 128), scales_ref[c], F32)
    return jnp.concatenate([1.0 / (s * s)] * (rows // 8), axis=0)


def lanes_sum(x):
    ones = jnp.ones((8, COLS), BF16)
    flat = x.reshape(CELLS, COLS).astype(BF16)
    return lax.dot_general(ones, flat, (((1,), (1,)), ((), ())), preferred_element_type=F32)


def part_of(part, block, lane):
    flat = block * 128 + lane
    return (flat >= part * (CELLS // M)) & (flat < (part + 1) * (CELLS // M))


def pack_kernel(scales_hbm, own_hbm, obs_hbm, pay_ref, aux_ref, scales_ref, own_ref, obs_ref, sems):
    me = lax.axis_index("y")
    per = C // PIECES
    get_scales = pltpu.make_async_copy(scales_hbm, scales_ref, sems.at[2 * PIECES])
    get_scales.start()
    copies = []
    for i in range(PIECES):
        part = pl.ds(i * per, per)
        copies.append(
            (
                pltpu.make_async_copy(own_hbm.at[0, part], own_ref.at[part], sems.at[2 * i]),
                pltpu.make_async_copy(obs_hbm.at[part], obs_ref.at[part], sems.at[2 * i + 1]),
            )
        )
        for copy in copies[-1]:
            copy.start()

    w = tile_weights((ROWS, 128))
    flat = iota((8, 128), 0) * 128 + iota((8, 128), 1)
    channel = lax.shift_right_logical(flat * 2731, 16)
    weight = row_weight(lat_index() * ROWS + flat - channel * ROWS)
    inv = jnp.zeros((8, 128), F32)
    get_scales.wait()
    for c in range(C):
        one = inverse_square(scales_ref, c)
        aux_ref[INV + c : INV + c + 1] = one[0:1]
        inv = jnp.where(channel == c, one, inv)
    aux_ref[8:16] = weight * inv * np.float32(1.0 / (C * SUMW * GROUP))

    total = jnp.zeros((ROWS, 128), F32)
    for i in range(PIECES):
        for copy in copies[i]:
            copy.wait()
        for c in range(i * per, (i + 1) * per):
            x = own_ref[c].astype(F32)
            d = x - obs_ref[c].astype(F32)
            d = d * d
            total = total + (d[:, :128] + d[:, 128:]) * inverse_square(scales_ref, c, ROWS)
            for h in range(2):
                pay_ref[2 * c + h, 0:16] = x[0:16, h * 128 : (h + 1) * 128].astype(BF16)
    total = total * w
    aux_ref[0:8] = (total[0:8] + total[8:16] + total[16:24]) * np.float32(1.0 / (C * LON * SUMW))

    x = own_ref[...].astype(F32)
    zx = lanes_sum(x)
    zy = lanes_sum(obs_ref[...].astype(F32))
    row, lane = iota((8, 128), 0), iota((8, 128), 1)

    def high(v):
        return v.astype(BF16).astype(F32)

    part = jnp.zeros((8, 128), F32)
    extra = jnp.zeros((8, 128), F32)
    for k in range(3):
        part = jnp.where(part_of(me, k, lane), zy[:, k * 128 : (k + 1) * 128], part)
        zk = zx[:, k * 128 : (k + 1) * 128]
        extra = jnp.where(row == k, high(zk), extra)
        extra = jnp.where(row == k + 3, zk - high(zk), extra)
    extra = jnp.where(row == 6, high(part), extra)
    extra = jnp.where(row == 7, part - high(part), extra)
    for d in range(GROUP):
        h = d % 2
        last = jnp.concatenate([x[d // 2, 16:24, h * 128 : (h + 1) * 128], extra], axis=0)
        pay_ref[d, 16:32] = last.astype(BF16)


def distance_kernel(recv_ref, aux_ref, msg_ref, zall_ref, token_ref, rows_ref):
    token_ref[...] = jnp.zeros((8, 128), F32)
    me = lax.axis_index("y")
    inv = aux_ref[pl.ds(INV + me * 2 + lax.axis_index("xl"), 1)]
    w = tile_weights((ROWS, 128)) * (inv * np.float32(1.0 / (C * LON * SUMW)))
    row, lane = iota((8, 128), 0), iota((8, 128), 1)
    got = [recv_ref[s].astype(F32) for s in range(GROUP)]
    rows_ref[...] = jnp.zeros((128, 128), F32)
    pairs = [(k, m, (m - k) % M) for k in (1, 2, 3, 4) for m in range(M) if k < 4 or m < 4]

    def put(at, value):
        rows_ref[at : at + 1] = jnp.sum(value, axis=0, keepdims=True)

    totals = [jnp.zeros((8, 128), F32) for _ in pairs]
    for t in range(3):
        rows8 = slice(t * 8, t * 8 + 8)
        for p, (_, m, n) in enumerate(pairs):
            acc = None
            for l in range(4):
                d = got[m * 4 + l][rows8] - got[n * 4 + l][rows8]
                acc = d * d if acc is None else acc + d * d
            totals[p] = totals[p] + acc * w[rows8]
    for p, (k, m, _) in enumerate(pairs):
        put((k - 1) * 8 + m, totals[p])
    rows_ref[32:40] = jnp.where(row == me, jnp.sum(aux_ref[0:8], axis=0, keepdims=True), 0.0)

    zw = aux_ref[8:16]
    real = row < 3
    zobs = jnp.zeros((8, 128), F32)
    zonal = []
    for m in range(M):
        s = sum(got[m * 4 + l][24:32] for l in range(4))
        z = jnp.where(real, s + jnp.concatenate([s[3:8], s[0:3]], axis=0), 0.0) * np.float32(1.0 / LON)
        zonal.append(z)
        zall_ref[m] = z
        part = s[6:7] + s[7:8]
        zobs = jnp.where(real & part_of(m, row, lane), part, zobs)
    zobs = zobs * np.float32(1.0 / LON)
    zall_ref[M] = zobs
    for k, m, n in pairs:
        d = zonal[m] - zonal[n]
        put(40 + (k - 1) * 8 + m, zw * d * d)
    for m in range(M):
        d = zonal[m] - zobs
        put(72 + m, zw * d * d)
    ones = jnp.ones((8, 128), F32)
    sums = lax.dot_general(
        ones, rows_ref[...], (((1,), (1,)), ((), ())), precision=HIGHEST, preferred_element_type=F32
    )
    msg_ref[...] = jnp.broadcast_to(sums[0:1][None], msg_ref.shape)


def relay_kernel(in_ref, out_ref):
    total = jnp.sum(in_ref[...], axis=0)
    out_ref[...] = jnp.broadcast_to(total[None], out_ref.shape)


def stack_kernel(own_ref, up_ref, down_ref, token_ref, ups_ref, downs_ref):
    ups_ref[0:C] = up_ref[...]
    ups_ref[C : 2 * C] = down_ref[...]
    ups_ref[2 * C :] = own_ref[0, 0:FIRST]
    downs_ref[0:C] = own_ref[0]
    downs_ref[C : 2 * C] = down_ref[...]
    downs_ref[2 * C :] = up_ref[FIRST:]


def coefficient_kernel(msg_ref, zall_ref, obs_ref, own_ref, down_ref, up_ref, coef_ref, begun_ref, zcol_ref):
    me = lax.axis_index("y")
    dist = jnp.sum(msg_ref[...], axis=0)
    row, lane = iota((16, 128), 0), iota((16, 128), 1)
    j = row & 7
    k = j + 1
    at = jnp.where(
        k <= 3,
        j * 8 + ((me + k) & 7),
        jnp.where(k == 4, 24 + (me & 3), jnp.where(k <= 7, (7 - k) * 8 + me, 32 + me)),
    )
    at = at + jnp.where(row >= 8, 40, 0)
    e = jnp.broadcast_to(jnp.exp(dist * np.float32(-0.5 / BAND)), (16, 128))
    picked = jnp.sum(jnp.where(lane == at, e, 0.0), axis=1, keepdims=True)
    norm = jnp.where(j == 7, 1.0 / (M * BAND), 1.0 / (M * (M - 1) * BAND))
    coef = jnp.broadcast_to(picked, (16, 128)) * norm
    coef_ref[...] = coef
    zme = zall_ref[me]
    z = coef[15:16] * (zme - zall_ref[M])
    for k in range(1, M):
        z = z + coef[7 + k : 8 + k] * (zall_ref[(me + k) & 7] - zme)
    for b in range(3):
        zcol_ref[b * 128 : (b + 1) * 128] = jnp.broadcast_to(z[b : b + 1], (128, 128)).T
    coef = jnp.concatenate([coef, coef], axis=1)
    for c in range(C):
        xm = own_ref[0, c].astype(F32)
        acc = coef[7:8] * (xm - obs_ref[c].astype(F32))
        acc = acc + coef[1:2] * (up_ref[c].astype(F32) - xm)
        acc = acc + coef[4:5] * (down_ref[c].astype(F32) - xm)
        z = zcol_ref[c * ROWS : (c + 1) * ROWS]
        begun_ref[c] = acc + jnp.concatenate([z, z], axis=1)


def mix_kernel(aux_ref, coef_ref, begun_ref, own_ref, ups_ref, downs_ref, out_hbm, out_ref, sems):
    def tile(k, c):
        if k == 1:
            return ups_ref[2 * C + c] if c < FIRST else downs_ref[2 * C + c - FIRST]
        return {3: ups_ref, 6: ups_ref, 7: downs_ref, 4: downs_ref}[k][c + (C if k in (6, 4) else 0)]

    fac = tile_weights((ROWS, 128)) * np.float32(LAT / SUMW)
    coef = coef_ref[...]
    coef = jnp.concatenate([coef, coef], axis=1)
    per = C // PARTS
    copies = []
    for c in range(C):
        xm = own_ref[0, c].astype(F32)
        acc = begun_ref[c]
        for k in (1, 3, 4, 6, 7):
            acc = acc + coef[k - 1 : k] * (tile(k, c).astype(F32) - xm)
        f = fac * aux_ref[INV + c : INV + c + 1]
        out_ref[c] = acc * jnp.concatenate([f, f], axis=1)
        if c % per == per - 1:
            part = pl.ds(c + 1 - per, per)
            copies.append(pltpu.make_async_copy(out_ref.at[part], out_hbm.at[0, part], sems.at[c // per]))
            copies[-1].start()
    for copy in copies:
        copy.wait()


VMEM = pl.BlockSpec(memory_space=pltpu.VMEM)
SMEM = pl.BlockSpec(memory_space=pltpu.SMEM)


def call(kernel, out_shape, in_specs, cost, vmem=32, **kw):
    return pl.pallas_call(
        kernel,
        out_shape=out_shape,
        in_specs=in_specs,
        cost_estimate=pl.CostEstimate(flops=cost, bytes_accessed=cost, transcendentals=0),
        compiler_params=pltpu.CompilerParams(vmem_limit_bytes=vmem * 1024 * 1024),
        **kw,
    )


def from_ahead(tile, k):
    return lax.ppermute(tile, "y", [((i + k) % M, i) for i in range(M)])


def per_device(members, observed, scales):
    shape = jax.ShapeDtypeStruct
    hbm = pl.BlockSpec(memory_space=pltpu.HBM)
    pay, aux = call(
        pack_kernel,
        (shape((GROUP, 32, 128), BF16), shape((INV + C, 128), F32)),
        [hbm] * 3,
        1 << 20,
        vmem=60,
        out_specs=(VMEM, VMEM),
        scratch_shapes=[
            pltpu.SMEM((C,), F32),
            pltpu.VMEM((C, ROWS, COLS), BF16),
            pltpu.VMEM((C, ROWS, COLS), BF16),
            pltpu.SemaphoreType.DMA((2 * PIECES + 1,)),
        ],
    )(scales, members, observed)
    recv = lax.all_to_all(pay, ("y", "xl", "core"), 0, 0, tiled=True)
    up, down = from_ahead(members[0], 2), from_ahead(members[0], -3)
    msg, zall, token = call(
        distance_kernel,
        (shape((128, 1, 128), F32), shape((16, 8, 128), F32), shape((8, 128), F32)),
        [VMEM, VMEM],
        LONG,
        out_specs=(VMEM, VMEM, VMEM),
        scratch_shapes=[pltpu.VMEM((128, 128), F32)],
    )(recv, aux)
    msg = lax.all_to_all(msg, ("y", "xh", "xl", "core"), 0, 0, tiled=True)
    stacks = tuple(shape((2 * C + n, ROWS, COLS), BF16) for n in (FIRST, C - FIRST))
    ups, downs = call(stack_kernel, stacks, [VMEM] * 4, 1 << 22, out_specs=(VMEM,) * 2)(
        members, up, down, token
    )
    ups, downs = from_ahead(ups, 1), from_ahead(downs, -1)
    msg = call(relay_kernel, shape((8, 1, 128), F32), [VMEM], LONG, out_specs=VMEM)(msg)
    msg = lax.all_to_all(msg, "z", 0, 0, tiled=True)
    coef, begun = call(
        coefficient_kernel,
        (shape((16, 128), F32), shape((C, ROWS, COLS), F32)),
        [VMEM] * 6,
        1 << 16,
        out_specs=(VMEM, VMEM),
        scratch_shapes=[pltpu.VMEM((CELLS, 128), F32)],
    )(msg, zall, observed, members, down, up)
    return call(
        mix_kernel,
        shape((1, C, ROWS, COLS), F32),
        [VMEM] * 6,
        1 << 22,
        out_specs=hbm,
        scratch_shapes=[pltpu.VMEM((C, ROWS, COLS), F32), pltpu.SemaphoreType.DMA((PARTS,))],
    )(aux, coef, begun, members, ups, downs)


def solution(mesh):
    fine = Mesh(mesh.devices.reshape(8, 8, 4, 2, 2), ("y", "z", "xh", "xl", "core"))
    placed = P("y", None, ("z", "xh"), ("xl", "core"))
    return jax.shard_map(
        per_device,
        mesh=fine,
        in_specs=(placed, P(None, ("z", "xh"), ("xl", "core")), P()),
        out_specs=placed,
        check_vma=False,
    )
```

```python
import functools

import jax
import jax.numpy as jnp
import numpy as np
from jax import lax
from jax.experimental import pallas as pl
from jax.experimental.pallas import tpu as pltpu
from jax.sharding import Mesh
from jax.sharding import PartitionSpec as P

BAND = 1.0
F32 = jnp.float32
BF16 = jnp.bfloat16
C, M, LAT, LON = 16, 8, 768, 1024
ROWS, COLS = 24, 256
CELLS = C * ROWS
FIRST = 8
INV = 16
PIECES = 4
PARTS = 8
GROUP = 32
LONG = 1 << 36
HIGHEST = lax.Precision.HIGHEST


def total_weight():
    index = np.arange(LAT).astype(np.float32)
    angle = (np.float32(-90.0) + (index + np.float32(0.5)) * np.float32(180.0) / np.float32(LAT)) * np.float32(
        np.pi / 180.0
    )
    return float(np.sum(np.cos(angle.astype(np.float32)).astype(np.float64)))


SUMW = total_weight()


def row_weight(index):
    angle = (-90.0 + (index.astype(F32) + 0.5) * 180.0 / LAT) * np.float32(np.pi / 180.0)
    return jnp.cos(angle)


def iota(shape, axis):
    return lax.broadcasted_iota(jnp.int32, shape, axis)


def lat_index():
    return lax.axis_index("z") * 4 + lax.axis_index("xh")


def tile_weights(shape):
    return row_weight(lat_index() * ROWS + iota(shape, 0))


def inverse_square(scales_ref, c, rows=8):
    s = jnp.full((8, 128), scales_ref[c], F32)
    return jnp.concatenate([1.0 / (s * s)] * (rows // 8), axis=0)


def lanes_sum(x):
    ones = jnp.ones((8, COLS), BF16)
    flat = x.reshape(CELLS, COLS).astype(BF16)
    return lax.dot_general(ones, flat, (((1,), (1,)), ((), ())), preferred_element_type=F32)


def part_of(part, block, lane):
    flat = block * 128 + lane
    return (flat >= part * (CELLS // M)) & (flat < (part + 1) * (CELLS // M))


def pack_kernel(scales_hbm, own_hbm, obs_hbm, pay_ref, aux_ref, scales_ref, own_ref, obs_ref, sems):
    me = lax.axis_index("y")
    per = C // PIECES
    get_scales = pltpu.make_async_copy(scales_hbm, scales_ref, sems.at[2 * PIECES])
    get_scales.start()
    copies = []
    for i in range(PIECES):
        part = pl.ds(i * per, per)
        copies.append(
            (
                pltpu.make_async_copy(own_hbm.at[0, part], own_ref.at[part], sems.at[2 * i]),
                pltpu.make_async_copy(obs_hbm.at[part], obs_ref.at[part], sems.at[2 * i + 1]),
            )
        )
        for copy in copies[-1]:
            copy.start()

    w = tile_weights((ROWS, 128))
    flat = iota((8, 128), 0) * 128 + iota((8, 128), 1)
    channel = lax.shift_right_logical(flat * 2731, 16)
    weight = row_weight(lat_index() * ROWS + flat - channel * ROWS)
    inv = jnp.zeros((8, 128), F32)
    get_scales.wait()
    for c in range(C):
        one = inverse_square(scales_ref, c)
        aux_ref[INV + c : INV + c + 1] = one[0:1]
        inv = jnp.where(channel == c, one, inv)
    aux_ref[8:16] = weight * inv * np.float32(1.0 / (C * SUMW * GROUP))

    total = jnp.zeros((ROWS, 128), F32)
    for i in range(PIECES):
        for copy in copies[i]:
            copy.wait()
        for c in range(i * per, (i + 1) * per):
            x = own_ref[c].astype(F32)
            d = x - obs_ref[c].astype(F32)
            d = d * d
            total = total + (d[:, :128] + d[:, 128:]) * inverse_square(scales_ref, c, ROWS)
            for h in range(2):
                pay_ref[2 * c + h, 0:16] = x[0:16, h * 128 : (h + 1) * 128].astype(BF16)
    total = total * w
    aux_ref[0:8] = (total[0:8] + total[8:16] + total[16:24]) * np.float32(1.0 / (C * LON * SUMW))

    x = own_ref[...].astype(F32)
    zx = lanes_sum(x)
    zy = lanes_sum(obs_ref[...].astype(F32))
    row, lane = iota((8, 128), 0), iota((8, 128), 1)

    def high(v):
        return v.astype(BF16).astype(F32)

    part = jnp.zeros((8, 128), F32)
    extra = jnp.zeros((8, 128), F32)
    for k in range(3):
        part = jnp.where(part_of(me, k, lane), zy[:, k * 128 : (k + 1) * 128], part)
        zk = zx[:, k * 128 : (k + 1) * 128]
        extra = jnp.where(row == k, high(zk), extra)
        extra = jnp.where(row == k + 3, zk - high(zk), extra)
    extra = jnp.where(row == 6, high(part), extra)
    extra = jnp.where(row == 7, part - high(part), extra)
    for d in range(GROUP):
        h = d % 2
        last = jnp.concatenate([x[d // 2, 16:24, h * 128 : (h + 1) * 128], extra], axis=0)
        pay_ref[d, 16:32] = last.astype(BF16)


def distance_kernel(recv_ref, aux_ref, msg_ref, zall_ref, token_ref, rows_ref):
    token_ref[...] = jnp.zeros((8, 128), F32)
    me = lax.axis_index("y")
    inv = aux_ref[pl.ds(INV + me * 2 + lax.axis_index("xl"), 1)]
    w = tile_weights((ROWS, 128)) * (inv * np.float32(1.0 / (C * LON * SUMW)))
    row, lane = iota((8, 128), 0), iota((8, 128), 1)
    got = [recv_ref[s].astype(F32) for s in range(GROUP)]
    rows_ref[...] = jnp.zeros((128, 128), F32)
    pairs = [(k, m, (m - k) % M) for k in (1, 2, 3, 4) for m in range(M) if k < 4 or m < 4]

    def put(at, value):
        rows_ref[at : at + 1] = jnp.sum(value, axis=0, keepdims=True)

    totals = [jnp.zeros((8, 128), F32) for _ in pairs]
    for t in range(3):
        rows8 = slice(t * 8, t * 8 + 8)
        for p, (_, m, n) in enumerate(pairs):
            acc = None
            for l in range(4):
                d = got[m * 4 + l][rows8] - got[n * 4 + l][rows8]
                acc = d * d if acc is None else acc + d * d
            totals[p] = totals[p] + acc * w[rows8]
    for p, (k, m, _) in enumerate(pairs):
        put((k - 1) * 8 + m, totals[p])
    rows_ref[32:40] = jnp.where(row == me, jnp.sum(aux_ref[0:8], axis=0, keepdims=True), 0.0)

    zw = aux_ref[8:16]
    real = row < 3
    zobs = jnp.zeros((8, 128), F32)
    zonal = []
    for m in range(M):
        s = sum(got[m * 4 + l][24:32] for l in range(4))
        z = jnp.where(real, s + jnp.concatenate([s[3:8], s[0:3]], axis=0), 0.0) * np.float32(1.0 / LON)
        zonal.append(z)
        zall_ref[m] = z
        part = s[6:7] + s[7:8]
        zobs = jnp.where(real & part_of(m, row, lane), part, zobs)
    zobs = zobs * np.float32(1.0 / LON)
    zall_ref[M] = zobs
    for k, m, n in pairs:
        d = zonal[m] - zonal[n]
        put(40 + (k - 1) * 8 + m, zw * d * d)
    for m in range(M):
        d = zonal[m] - zobs
        put(72 + m, zw * d * d)
    ones = jnp.ones((8, 128), F32)
    sums = lax.dot_general(
        ones, rows_ref[...], (((1,), (1,)), ((), ())), precision=HIGHEST, preferred_element_type=F32
    )
    msg_ref[...] = jnp.broadcast_to(sums[0:1][None], msg_ref.shape)


def relay_kernel(in_ref, out_ref):
    total = jnp.sum(in_ref[...], axis=0)
    out_ref[...] = jnp.broadcast_to(total[None], out_ref.shape)


def stack_kernel(own_ref, up_ref, down_ref, token_ref, ups_ref, downs_ref):
    ups_ref[0:C] = up_ref[...]
    ups_ref[C : 2 * C] = down_ref[...]
    ups_ref[2 * C :] = own_ref[0, 0:FIRST]
    downs_ref[0:C] = own_ref[0]
    downs_ref[C : 2 * C] = down_ref[...]
    downs_ref[2 * C :] = up_ref[FIRST:]


def coefficient_kernel(msg_ref, zall_ref, obs_ref, own_ref, down_ref, up_ref, coef_ref, begun_ref, zcol_ref):
    me = lax.axis_index("y")
    dist = jnp.sum(msg_ref[...], axis=0)
    row, lane = iota((16, 128), 0), iota((16, 128), 1)
    j = row & 7
    k = j + 1
    at = jnp.where(
        k <= 3,
        j * 8 + ((me + k) & 7),
        jnp.where(k == 4, 24 + (me & 3), jnp.where(k <= 7, (7 - k) * 8 + me, 32 + me)),
    )
    at = at + jnp.where(row >= 8, 40, 0)
    e = jnp.broadcast_to(jnp.exp(dist * np.float32(-0.5 / BAND)), (16, 128))
    picked = jnp.sum(jnp.where(lane == at, e, 0.0), axis=1, keepdims=True)
    norm = jnp.where(j == 7, 1.0 / (M * BAND), 1.0 / (M * (M - 1) * BAND))
    coef = jnp.broadcast_to(picked, (16, 128)) * norm
    coef_ref[...] = coef
    zme = zall_ref[me]
    z = coef[15:16] * (zme - zall_ref[M])
    for k in range(1, M):
        z = z + coef[7 + k : 8 + k] * (zall_ref[(me + k) & 7] - zme)
    for b in range(3):
        zcol_ref[b * 128 : (b + 1) * 128] = jnp.broadcast_to(z[b : b + 1], (128, 128)).T
    coef = jnp.concatenate([coef, coef], axis=1)
    for c in range(C):
        xm = own_ref[0, c].astype(F32)
        acc = coef[7:8] * (xm - obs_ref[c].astype(F32))
        acc = acc + coef[1:2] * (up_ref[c].astype(F32) - xm)
        acc = acc + coef[4:5] * (down_ref[c].astype(F32) - xm)
        z = zcol_ref[c * ROWS : (c + 1) * ROWS]
        begun_ref[c] = acc + jnp.concatenate([z, z], axis=1)


def mix_kernel(aux_ref, coef_ref, begun_ref, own_ref, ups_ref, downs_ref, out_hbm, out_ref, sems):
    def tile(k, c):
        if k == 1:
            return ups_ref[2 * C + c] if c < FIRST else downs_ref[2 * C + c - FIRST]
        return {3: ups_ref, 6: ups_ref, 7: downs_ref, 4: downs_ref}[k][c + (C if k in (6, 4) else 0)]

    fac = tile_weights((ROWS, 128)) * np.float32(LAT / SUMW)
    coef = coef_ref[...]
    coef = jnp.concatenate([coef, coef], axis=1)
    per = C // PARTS
    copies = []
    for c in range(C):
        xm = own_ref[0, c].astype(F32)
        acc = begun_ref[c]
        for k in (1, 3, 4, 6, 7):
            acc = acc + coef[k - 1 : k] * (tile(k, c).astype(F32) - xm)
        f = fac * aux_ref[INV + c : INV + c + 1]
        out_ref[c] = acc * jnp.concatenate([f, f], axis=1)
        if c % per == per - 1:
            part = pl.ds(c + 1 - per, per)
            copies.append(pltpu.make_async_copy(out_ref.at[part], out_hbm.at[0, part], sems.at[c // per]))
            copies[-1].start()
    for copy in copies:
        copy.wait()


VMEM = pl.BlockSpec(memory_space=pltpu.VMEM)
SMEM = pl.BlockSpec(memory_space=pltpu.SMEM)


def call(kernel, out_shape, in_specs, cost, vmem=32, **kw):
    return pl.pallas_call(
        kernel,
        out_shape=out_shape,
        in_specs=in_specs,
        cost_estimate=pl.CostEstimate(flops=cost, bytes_accessed=cost, transcendentals=0),
        compiler_params=pltpu.CompilerParams(vmem_limit_bytes=vmem * 1024 * 1024),
        **kw,
    )


def from_ahead(tile, k):
    return lax.ppermute(tile, "y", [((i + k) % M, i) for i in range(M)])


def per_device(members, observed, scales):
    shape = jax.ShapeDtypeStruct
    hbm = pl.BlockSpec(memory_space=pltpu.HBM)
    pay, aux = call(
        pack_kernel,
        (shape((GROUP, 32, 128), BF16), shape((INV + C, 128), F32)),
        [hbm] * 3,
        1 << 20,
        vmem=60,
        out_specs=(VMEM, VMEM),
        scratch_shapes=[
            pltpu.SMEM((C,), F32),
            pltpu.VMEM((C, ROWS, COLS), BF16),
            pltpu.VMEM((C, ROWS, COLS), BF16),
            pltpu.SemaphoreType.DMA((2 * PIECES + 1,)),
        ],
    )(scales, members, observed)
    recv = lax.all_to_all(pay, ("y", "xl", "core"), 0, 0, tiled=True)
    up, down = from_ahead(members[0], 2), from_ahead(members[0], -3)
    msg, zall, token = call(
        distance_kernel,
        (shape((64, 1, 128), F32), shape((16, 8, 128), F32), shape((8, 128), F32)),
        [VMEM, VMEM],
        LONG,
        out_specs=(VMEM, VMEM, VMEM),
        scratch_shapes=[pltpu.VMEM((128, 128), F32)],
    )(recv, aux)
    msg = lax.all_to_all(msg, ("y", "xh", "xl"), 0, 0, tiled=True)
    stacks = tuple(shape((2 * C + n, ROWS, COLS), BF16) for n in (FIRST, C - FIRST))
    ups, downs = call(stack_kernel, stacks, [VMEM] * 4, 1 << 22, out_specs=(VMEM,) * 2)(
        members, up, down, token
    )
    ups, downs = from_ahead(ups, 1), from_ahead(downs, -1)
    msg = call(relay_kernel, shape((16, 1, 128), F32), [VMEM], LONG, out_specs=VMEM)(msg)
    msg = lax.all_to_all(msg, ("z", "core"), 0, 0, tiled=True)
    coef, begun = call(
        coefficient_kernel,
        (shape((16, 128), F32), shape((C, ROWS, COLS), F32)),
        [VMEM] * 6,
        1 << 16,
        out_specs=(VMEM, VMEM),
        scratch_shapes=[pltpu.VMEM((CELLS, 128), F32)],
    )(msg, zall, observed, members, down, up)
    return call(
        mix_kernel,
        shape((1, C, ROWS, COLS), F32),
        [VMEM] * 6,
        1 << 22,
        out_specs=hbm,
        scratch_shapes=[pltpu.VMEM((C, ROWS, COLS), F32), pltpu.SemaphoreType.DMA((PARTS,))],
    )(aux, coef, begun, members, ups, downs)


def solution(mesh):
    fine = Mesh(mesh.devices.reshape(8, 8, 4, 2, 2), ("y", "z", "xh", "xl", "core"))
    placed = P("y", None, ("z", "xh"), ("xl", "core"))
    return jax.shard_map(
        per_device,
        mesh=fine,
        in_specs=(placed, P(None, ("z", "xh"), ("xl", "core")), P()),
        out_specs=placed,
        check_vma=False,
    )
```

```python
import functools

import jax
import jax.numpy as jnp
import numpy as np
from jax import lax
from jax.experimental import pallas as pl
from jax.experimental.pallas import tpu as pltpu
from jax.sharding import Mesh
from jax.sharding import PartitionSpec as P

BAND = 1.0
F32 = jnp.float32
BF16 = jnp.bfloat16
C, M, LAT, LON = 16, 8, 768, 1024
ROWS, COLS = 24, 256
CELLS = C * ROWS
FIRST = 8
INV = 16
PIECES = 4
PARTS = 8
GROUP = 32
LONG = 1 << 36
HIGHEST = lax.Precision.HIGHEST


def total_weight():
    index = np.arange(LAT).astype(np.float32)
    angle = (np.float32(-90.0) + (index + np.float32(0.5)) * np.float32(180.0) / np.float32(LAT)) * np.float32(
        np.pi / 180.0
    )
    return float(np.sum(np.cos(angle.astype(np.float32)).astype(np.float64)))


SUMW = total_weight()


def row_weight(index):
    angle = (-90.0 + (index.astype(F32) + 0.5) * 180.0 / LAT) * np.float32(np.pi / 180.0)
    return jnp.cos(angle)


def iota(shape, axis):
    return lax.broadcasted_iota(jnp.int32, shape, axis)


def lat_index():
    return lax.axis_index("z") * 4 + lax.axis_index("xh")


def tile_weights(shape):
    return row_weight(lat_index() * ROWS + iota(shape, 0))


def inverse_square(scales_ref, c, rows=8):
    s = jnp.full((8, 128), scales_ref[c], F32)
    return jnp.concatenate([1.0 / (s * s)] * (rows // 8), axis=0)


def lanes_sum(x):
    ones = jnp.ones((8, COLS), BF16)
    flat = x.reshape(CELLS, COLS).astype(BF16)
    return lax.dot_general(ones, flat, (((1,), (1,)), ((), ())), preferred_element_type=F32)


def pack_kernel(scales_hbm, own_hbm, obs_hbm, pay_ref, aux_ref, scales_ref, own_ref, obs_ref, sems):
    per = C // PIECES
    get_scales = pltpu.make_async_copy(scales_hbm, scales_ref, sems.at[2 * PIECES])
    get_scales.start()
    copies = []
    for i in range(PIECES):
        part = pl.ds(i * per, per)
        copies.append(
            (
                pltpu.make_async_copy(own_hbm.at[0, part], own_ref.at[part], sems.at[2 * i]),
                pltpu.make_async_copy(obs_hbm.at[part], obs_ref.at[part], sems.at[2 * i + 1]),
            )
        )
        for copy in copies[-1]:
            copy.start()

    w = tile_weights((ROWS, 128))
    flat = iota((8, 128), 0) * 128 + iota((8, 128), 1)
    channel = lax.shift_right_logical(flat * 2731, 16)
    weight = row_weight(lat_index() * ROWS + flat - channel * ROWS)
    inv = jnp.zeros((8, 128), F32)
    get_scales.wait()
    for c in range(C):
        one = inverse_square(scales_ref, c)
        aux_ref[INV + c : INV + c + 1] = one[0:1]
        inv = jnp.where(channel == c, one, inv)
    aux_ref[8:16] = weight * inv * np.float32(1.0 / (C * SUMW * GROUP))

    total = jnp.zeros((ROWS, 128), F32)
    for i in range(PIECES):
        for copy in copies[i]:
            copy.wait()
        for c in range(i * per, (i + 1) * per):
            x = own_ref[c].astype(F32)
            d = x - obs_ref[c].astype(F32)
            d = d * d
            total = total + (d[:, :128] + d[:, 128:]) * inverse_square(scales_ref, c, ROWS)
            for h in range(2):
                pay_ref[2 * c + h, 0:16] = x[0:16, h * 128 : (h + 1) * 128].astype(BF16)
    total = total * w
    aux_ref[0:8] = (total[0:8] + total[8:16] + total[16:24]) * np.float32(1.0 / (C * LON * SUMW))

    x = own_ref[...].astype(F32)
    above = lanes_sum(x) - lanes_sum(obs_ref[...].astype(F32))
    row = iota((8, 128), 0)
    extra = jnp.zeros((8, 128), F32)
    for k in range(3):
        z = above[:, k * 128 : (k + 1) * 128]
        high = z.astype(BF16).astype(F32)
        extra = jnp.where(row == k, high, jnp.where(row == k + 3, z - high, extra))
    for d in range(GROUP):
        h = d % 2
        last = jnp.concatenate([x[d // 2, 16:24, h * 128 : (h + 1) * 128], extra], axis=0)
        pay_ref[d, 16:32] = last.astype(BF16)


def distance_kernel(recv_ref, aux_ref, msg_ref, zall_ref, token_ref, rows_ref):
    token_ref[...] = jnp.zeros((8, 128), F32)
    me = lax.axis_index("y")
    inv = aux_ref[pl.ds(INV + me * 2 + lax.axis_index("xl"), 1)]
    w = tile_weights((ROWS, 128)) * (inv * np.float32(1.0 / (C * LON * SUMW)))
    row = iota((8, 128), 0)
    got = [recv_ref[s].astype(F32) for s in range(GROUP)]
    rows_ref[...] = jnp.zeros((128, 128), F32)
    pairs = [(k, m, (m - k) % M) for k in (1, 2, 3, 4) for m in range(M) if k < 4 or m < 4]

    def put(at, value):
        rows_ref[at : at + 1] = jnp.sum(value, axis=0, keepdims=True)

    totals = [jnp.zeros((8, 128), F32) for _ in pairs]
    for t in range(3):
        rows8 = slice(t * 8, t * 8 + 8)
        for p, (_, m, n) in enumerate(pairs):
            acc = None
            for l in range(4):
                d = got[m * 4 + l][rows8] - got[n * 4 + l][rows8]
                acc = d * d if acc is None else acc + d * d
            totals[p] = totals[p] + acc * w[rows8]
    for p, (k, m, _) in enumerate(pairs):
        put((k - 1) * 8 + m, totals[p])
    rows_ref[32:40] = jnp.where(row == me, jnp.sum(aux_ref[0:8], axis=0, keepdims=True), 0.0)

    zw = aux_ref[8:16]
    real = row < 3
    zonal = []
    for m in range(M):
        s = sum(got[m * 4 + l][24:32] for l in range(4))
        z = jnp.where(real, s + jnp.concatenate([s[3:8], s[0:3]], axis=0), 0.0) * np.float32(1.0 / LON)
        zonal.append(z)
        zall_ref[m] = z
    for k, m, n in pairs:
        d = zonal[m] - zonal[n]
        put(40 + (k - 1) * 8 + m, zw * d * d)
    for m in range(M):
        put(72 + m, zw * zonal[m] * zonal[m])
    ones = jnp.ones((8, 128), F32)
    sums = lax.dot_general(
        ones, rows_ref[...], (((1,), (1,)), ((), ())), precision=HIGHEST, preferred_element_type=F32
    )
    msg_ref[...] = jnp.broadcast_to(sums[0:1][None], msg_ref.shape)


def relay_kernel(in_ref, out_ref):
    total = jnp.sum(in_ref[...], axis=0)
    out_ref[...] = jnp.broadcast_to(total[None], out_ref.shape)


def stack_kernel(own_ref, up_ref, down_ref, token_ref, ups_ref, downs_ref):
    ups_ref[0:C] = up_ref[...]
    ups_ref[C : 2 * C] = down_ref[...]
    ups_ref[2 * C :] = own_ref[0, 0:FIRST]
    downs_ref[0:C] = own_ref[0]
    downs_ref[C : 2 * C] = down_ref[...]
    downs_ref[2 * C :] = up_ref[FIRST:]


def coefficient_kernel(msg_ref, zall_ref, obs_ref, own_ref, down_ref, up_ref, coef_ref, begun_ref, zcol_ref):
    me = lax.axis_index("y")
    dist = jnp.sum(msg_ref[...], axis=0)
    row, lane = iota((16, 128), 0), iota((16, 128), 1)
    j = row & 7
    k = j + 1
    at = jnp.where(
        k <= 3,
        j * 8 + ((me + k) & 7),
        jnp.where(k == 4, 24 + (me & 3), jnp.where(k <= 7, (7 - k) * 8 + me, 32 + me)),
    )
    at = at + jnp.where(row >= 8, 40, 0)
    e = jnp.broadcast_to(jnp.exp(dist * np.float32(-0.5 / BAND)), (16, 128))
    picked = jnp.sum(jnp.where(lane == at, e, 0.0), axis=1, keepdims=True)
    norm = jnp.where(j == 7, 1.0 / (M * BAND), 1.0 / (M * (M - 1) * BAND))
    coef = jnp.broadcast_to(picked, (16, 128)) * norm
    coef_ref[...] = coef
    zme = zall_ref[me]
    z = coef[15:16] * zme
    for k in range(1, M):
        z = z + coef[7 + k : 8 + k] * (zall_ref[(me + k) & 7] - zme)
    for b in range(3):
        zcol_ref[b * 128 : (b + 1) * 128] = jnp.broadcast_to(z[b : b + 1], (128, 128)).T
    coef = jnp.concatenate([coef, coef], axis=1)
    for c in range(C):
        xm = own_ref[0, c].astype(F32)
        acc = coef[7:8] * (xm - obs_ref[c].astype(F32))
        acc = acc + coef[1:2] * (up_ref[c].astype(F32) - xm)
        acc = acc + coef[4:5] * (down_ref[c].astype(F32) - xm)
        z = zcol_ref[c * ROWS : (c + 1) * ROWS]
        begun_ref[c] = acc + jnp.concatenate([z, z], axis=1)


def mix_kernel(aux_ref, coef_ref, begun_ref, own_ref, ups_ref, downs_ref, out_hbm, out_ref, sems):
    def tile(k, c):
        if k == 1:
            return ups_ref[2 * C + c] if c < FIRST else downs_ref[2 * C + c - FIRST]
        return {3: ups_ref, 6: ups_ref, 7: downs_ref, 4: downs_ref}[k][c + (C if k in (6, 4) else 0)]

    fac = tile_weights((ROWS, 128)) * np.float32(LAT / SUMW)
    coef = coef_ref[...]
    coef = jnp.concatenate([coef, coef], axis=1)
    per = C // PARTS
    copies = []
    for c in range(C):
        xm = own_ref[0, c].astype(F32)
        acc = begun_ref[c]
        for k in (1, 3, 4, 6, 7):
            acc = acc + coef[k - 1 : k] * (tile(k, c).astype(F32) - xm)
        f = fac * aux_ref[INV + c : INV + c + 1]
        out_ref[c] = acc * jnp.concatenate([f, f], axis=1)
        if c % per == per - 1:
            part = pl.ds(c + 1 - per, per)
            copies.append(pltpu.make_async_copy(out_ref.at[part], out_hbm.at[0, part], sems.at[c // per]))
            copies[-1].start()
    for copy in copies:
        copy.wait()


VMEM = pl.BlockSpec(memory_space=pltpu.VMEM)
SMEM = pl.BlockSpec(memory_space=pltpu.SMEM)


def call(kernel, out_shape, in_specs, cost, vmem=32, **kw):
    return pl.pallas_call(
        kernel,
        out_shape=out_shape,
        in_specs=in_specs,
        cost_estimate=pl.CostEstimate(flops=cost, bytes_accessed=cost, transcendentals=0),
        compiler_params=pltpu.CompilerParams(vmem_limit_bytes=vmem * 1024 * 1024),
        **kw,
    )


def from_ahead(tile, k):
    return lax.ppermute(tile, "y", [((i + k) % M, i) for i in range(M)])


def per_device(members, observed, scales):
    shape = jax.ShapeDtypeStruct
    hbm = pl.BlockSpec(memory_space=pltpu.HBM)
    pay, aux = call(
        pack_kernel,
        (shape((GROUP, 32, 128), BF16), shape((INV + C, 128), F32)),
        [hbm] * 3,
        1 << 20,
        vmem=60,
        out_specs=(VMEM, VMEM),
        scratch_shapes=[
            pltpu.SMEM((C,), F32),
            pltpu.VMEM((C, ROWS, COLS), BF16),
            pltpu.VMEM((C, ROWS, COLS), BF16),
            pltpu.SemaphoreType.DMA((2 * PIECES + 1,)),
        ],
    )(scales, members, observed)
    recv = lax.all_to_all(pay, ("y", "xl", "core"), 0, 0, tiled=True)
    up, down = from_ahead(members[0], 2), from_ahead(members[0], -3)
    msg, zall, token = call(
        distance_kernel,
        (shape((128, 1, 128), F32), shape((M, 8, 128), F32), shape((8, 128), F32)),
        [VMEM, VMEM],
        LONG,
        out_specs=(VMEM, VMEM, VMEM),
        scratch_shapes=[pltpu.VMEM((128, 128), F32)],
    )(recv, aux)
    msg = lax.all_to_all(msg, ("y", "xh", "xl", "core"), 0, 0, tiled=True)
    stacks = tuple(shape((2 * C + n, ROWS, COLS), BF16) for n in (FIRST, C - FIRST))
    ups, downs = call(stack_kernel, stacks, [VMEM] * 4, 1 << 22, out_specs=(VMEM,) * 2)(
        members, up, down, token
    )
    ups, downs = from_ahead(ups, 1), from_ahead(downs, -1)
    msg = call(relay_kernel, shape((8, 1, 128), F32), [VMEM], LONG, out_specs=VMEM)(msg)
    msg = lax.all_to_all(msg, "z", 0, 0, tiled=True)
    coef, begun = call(
        coefficient_kernel,
        (shape((16, 128), F32), shape((C, ROWS, COLS), F32)),
        [VMEM] * 6,
        1 << 16,
        out_specs=(VMEM, VMEM),
        scratch_shapes=[pltpu.VMEM((CELLS, 128), F32)],
    )(msg, zall, observed, members, down, up)
    return call(
        mix_kernel,
        shape((1, C, ROWS, COLS), F32),
        [VMEM] * 6,
        1 << 22,
        out_specs=hbm,
        scratch_shapes=[pltpu.VMEM((C, ROWS, COLS), F32), pltpu.SemaphoreType.DMA((PARTS,))],
    )(aux, coef, begun, members, ups, downs)


def solution(mesh):
    fine = Mesh(mesh.devices.reshape(8, 8, 4, 2, 2), ("y", "z", "xh", "xl", "core"))
    placed = P("y", None, ("z", "xh"), ("xl", "core"))
    return jax.shard_map(
        per_device,
        mesh=fine,
        in_specs=(placed, P(None, ("z", "xh"), ("xl", "core")), P()),
        out_specs=placed,
        check_vma=False,
    )
```

```python
import functools

import jax
import jax.numpy as jnp
import numpy as np
from jax import lax
from jax.experimental import pallas as pl
from jax.experimental.pallas import tpu as pltpu
from jax.sharding import Mesh
from jax.sharding import PartitionSpec as P

BAND = 1.0
F32 = jnp.float32
BF16 = jnp.bfloat16
C, M, LAT, LON = 16, 8, 768, 1024
ROWS, COLS = 24, 256
CELLS = C * ROWS
INV = 16
PIECES = 4
PARTS = 8
GROUP = 32
LONG = 1 << 36
HIGHEST = lax.Precision.HIGHEST


def total_weight():
    index = np.arange(LAT).astype(np.float32)
    angle = (np.float32(-90.0) + (index + np.float32(0.5)) * np.float32(180.0) / np.float32(LAT)) * np.float32(
        np.pi / 180.0
    )
    return float(np.sum(np.cos(angle.astype(np.float32)).astype(np.float64)))


SUMW = total_weight()


def row_weight(index):
    angle = (-90.0 + (index.astype(F32) + 0.5) * 180.0 / LAT) * np.float32(np.pi / 180.0)
    return jnp.cos(angle)


def iota(shape, axis):
    return lax.broadcasted_iota(jnp.int32, shape, axis)


def lat_index():
    return lax.axis_index("z") * 4 + lax.axis_index("xh")


def tile_weights(shape):
    return row_weight(lat_index() * ROWS + iota(shape, 0))


def inverse_square(scales_ref, c, rows=8):
    s = jnp.full((8, 128), scales_ref[c], F32)
    return jnp.concatenate([1.0 / (s * s)] * (rows // 8), axis=0)


def lanes_sum(x):
    ones = jnp.ones((8, COLS), BF16)
    flat = x.reshape(CELLS, COLS).astype(BF16)
    return lax.dot_general(ones, flat, (((1,), (1,)), ((), ())), preferred_element_type=F32)


def pack_kernel(scales_hbm, own_hbm, obs_hbm, pay_ref, aux_ref, scales_ref, own_ref, obs_ref, sems):
    per = C // PIECES
    get_scales = pltpu.make_async_copy(scales_hbm, scales_ref, sems.at[2 * PIECES])
    get_scales.start()
    copies = []
    for i in range(PIECES):
        part = pl.ds(i * per, per)
        copies.append(
            (
                pltpu.make_async_copy(own_hbm.at[0, part], own_ref.at[part], sems.at[2 * i]),
                pltpu.make_async_copy(obs_hbm.at[part], obs_ref.at[part], sems.at[2 * i + 1]),
            )
        )
        for copy in copies[-1]:
            copy.start()

    w = tile_weights((ROWS, 128))
    flat = iota((8, 128), 0) * 128 + iota((8, 128), 1)
    channel = lax.shift_right_logical(flat * 2731, 16)
    weight = row_weight(lat_index() * ROWS + flat - channel * ROWS)
    inv = jnp.zeros((8, 128), F32)
    get_scales.wait()
    for c in range(C):
        one = inverse_square(scales_ref, c)
        aux_ref[INV + c : INV + c + 1] = one[0:1]
        inv = jnp.where(channel == c, one, inv)
    aux_ref[8:16] = weight * inv * np.float32(1.0 / (C * SUMW * GROUP))

    total = jnp.zeros((ROWS, 128), F32)
    for i in range(PIECES):
        for copy in copies[i]:
            copy.wait()
        for c in range(i * per, (i + 1) * per):
            x = own_ref[c].astype(F32)
            d = x - obs_ref[c].astype(F32)
            d = d * d
            total = total + (d[:, :128] + d[:, 128:]) * inverse_square(scales_ref, c, ROWS)
            for h in range(2):
                pay_ref[2 * c + h, 0:16] = x[0:16, h * 128 : (h + 1) * 128].astype(BF16)
    total = total * w
    aux_ref[0:8] = (total[0:8] + total[8:16] + total[16:24]) * np.float32(1.0 / (C * LON * SUMW))

    x = own_ref[...].astype(F32)
    above = lanes_sum(x) - lanes_sum(obs_ref[...].astype(F32))
    row = iota((8, 128), 0)
    extra = jnp.zeros((8, 128), F32)
    for k in range(3):
        z = above[:, k * 128 : (k + 1) * 128]
        high = z.astype(BF16).astype(F32)
        extra = jnp.where(row == k, high, jnp.where(row == k + 3, z - high, extra))
    for d in range(GROUP):
        h = d % 2
        last = jnp.concatenate([x[d // 2, 16:24, h * 128 : (h + 1) * 128], extra], axis=0)
        pay_ref[d, 16:32] = last.astype(BF16)


def distance_kernel(recv_ref, aux_ref, msg_ref, zall_ref, token_ref, rows_ref):
    token_ref[...] = jnp.zeros((8, 128), F32)
    me = lax.axis_index("y")
    inv = aux_ref[pl.ds(INV + me * 2 + lax.axis_index("xl"), 1)]
    w = tile_weights((ROWS, 128)) * (inv * np.float32(1.0 / (C * LON * SUMW)))
    row = iota((8, 128), 0)
    got = [recv_ref[s].astype(F32) for s in range(GROUP)]
    rows_ref[...] = jnp.zeros((128, 128), F32)
    pairs = [(k, m, (m - k) % M) for k in (1, 2, 3, 4) for m in range(M) if k < 4 or m < 4]

    def put(at, value):
        rows_ref[at : at + 1] = jnp.sum(value, axis=0, keepdims=True)

    totals = [jnp.zeros((8, 128), F32) for _ in pairs]
    for t in range(3):
        rows8 = slice(t * 8, t * 8 + 8)
        for p, (_, m, n) in enumerate(pairs):
            acc = None
            for l in range(4):
                d = got[m * 4 + l][rows8] - got[n * 4 + l][rows8]
                acc = d * d if acc is None else acc + d * d
            totals[p] = totals[p] + acc * w[rows8]
    for p, (k, m, _) in enumerate(pairs):
        put((k - 1) * 8 + m, totals[p])
    rows_ref[32:40] = jnp.where(row == me, jnp.sum(aux_ref[0:8], axis=0, keepdims=True), 0.0)

    zw = aux_ref[8:16]
    real = row < 3
    zonal = []
    for m in range(M):
        s = sum(got[m * 4 + l][24:32] for l in range(4))
        z = jnp.where(real, s + jnp.concatenate([s[3:8], s[0:3]], axis=0), 0.0) * np.float32(1.0 / LON)
        zonal.append(z)
        zall_ref[m] = z
    for k, m, n in pairs:
        d = zonal[m] - zonal[n]
        put(40 + (k - 1) * 8 + m, zw * d * d)
    for m in range(M):
        put(72 + m, zw * zonal[m] * zonal[m])
    ones = jnp.ones((8, 128), F32)
    sums = lax.dot_general(
        ones, rows_ref[...], (((1,), (1,)), ((), ())), precision=HIGHEST, preferred_element_type=F32
    )
    msg_ref[...] = jnp.broadcast_to(sums[0:1][None], msg_ref.shape)


def relay_kernel(in_ref, out_ref):
    total = jnp.sum(in_ref[...], axis=0)
    out_ref[...] = jnp.broadcast_to(total[None], out_ref.shape)


def stack_kernel(own_ref, up_ref, down_ref, token_ref, ups_ref, downs_ref, again_ref):
    ups_ref[0:C] = own_ref[0]
    ups_ref[C : 2 * C] = up_ref[...]
    downs_ref[0:C] = own_ref[0]
    downs_ref[C : 2 * C] = down_ref[...]
    again_ref[...] = up_ref[...]


def coefficient_kernel(msg_ref, zall_ref, obs_ref, own_ref, down_ref, up_ref, coef_ref, begun_ref, zcol_ref):
    me = lax.axis_index("y")
    dist = jnp.sum(msg_ref[...], axis=0)
    row, lane = iota((16, 128), 0), iota((16, 128), 1)
    j = row & 7
    k = j + 1
    at = jnp.where(
        k <= 3,
        j * 8 + ((me + k) & 7),
        jnp.where(k == 4, 24 + (me & 3), jnp.where(k <= 7, (7 - k) * 8 + me, 32 + me)),
    )
    at = at + jnp.where(row >= 8, 40, 0)
    e = jnp.broadcast_to(jnp.exp(dist * np.float32(-0.5 / BAND)), (16, 128))
    picked = jnp.sum(jnp.where(lane == at, e, 0.0), axis=1, keepdims=True)
    norm = jnp.where(j == 7, 1.0 / (M * BAND), 1.0 / (M * (M - 1) * BAND))
    coef = jnp.broadcast_to(picked, (16, 128)) * norm
    coef_ref[...] = coef
    zme = zall_ref[me]
    z = coef[15:16] * zme
    for k in range(1, M):
        z = z + coef[7 + k : 8 + k] * (zall_ref[(me + k) & 7] - zme)
    for b in range(3):
        zcol_ref[b * 128 : (b + 1) * 128] = jnp.broadcast_to(z[b : b + 1], (128, 128)).T
    coef = jnp.concatenate([coef, coef], axis=1)
    for c in range(C):
        xm = own_ref[0, c].astype(F32)
        acc = coef[7:8] * (xm - obs_ref[c].astype(F32))
        acc = acc + coef[1:2] * (up_ref[c].astype(F32) - xm)
        acc = acc + coef[5:6] * (down_ref[c].astype(F32) - xm)
        z = zcol_ref[c * ROWS : (c + 1) * ROWS]
        begun_ref[c] = acc + jnp.concatenate([z, z], axis=1)


def mix_kernel(aux_ref, coef_ref, begun_ref, own_ref, ups_ref, downs_ref, again_ref, out_hbm, out_ref, sems):
    def tile(k, c):
        return {1: ups_ref, 3: ups_ref, 7: downs_ref, 5: downs_ref, 4: again_ref}[k][c + (C if k in (3, 5) else 0)]

    fac = tile_weights((ROWS, 128)) * np.float32(LAT / SUMW)
    coef = coef_ref[...]
    coef = jnp.concatenate([coef, coef], axis=1)
    per = C // PARTS
    copies = []
    for c in range(C):
        xm = own_ref[0, c].astype(F32)
        acc = begun_ref[c]
        for k in (1, 3, 4, 5, 7):
            acc = acc + coef[k - 1 : k] * (tile(k, c).astype(F32) - xm)
        f = fac * aux_ref[INV + c : INV + c + 1]
        out_ref[c] = acc * jnp.concatenate([f, f], axis=1)
        if c % per == per - 1:
            part = pl.ds(c + 1 - per, per)
            copies.append(pltpu.make_async_copy(out_ref.at[part], out_hbm.at[0, part], sems.at[c // per]))
            copies[-1].start()
    for copy in copies:
        copy.wait()


VMEM = pl.BlockSpec(memory_space=pltpu.VMEM)
SMEM = pl.BlockSpec(memory_space=pltpu.SMEM)


def call(kernel, out_shape, in_specs, cost, vmem=32, **kw):
    return pl.pallas_call(
        kernel,
        out_shape=out_shape,
        in_specs=in_specs,
        cost_estimate=pl.CostEstimate(flops=cost, bytes_accessed=cost, transcendentals=0),
        compiler_params=pltpu.CompilerParams(vmem_limit_bytes=vmem * 1024 * 1024),
        **kw,
    )


def from_ahead(tile, k):
    return lax.ppermute(tile, "y", [((i + k) % M, i) for i in range(M)])


def per_device(members, observed, scales):
    shape = jax.ShapeDtypeStruct
    hbm = pl.BlockSpec(memory_space=pltpu.HBM)
    pay, aux = call(
        pack_kernel,
        (shape((GROUP, 32, 128), BF16), shape((INV + C, 128), F32)),
        [hbm] * 3,
        1 << 20,
        vmem=60,
        out_specs=(VMEM, VMEM),
        scratch_shapes=[
            pltpu.SMEM((C,), F32),
            pltpu.VMEM((C, ROWS, COLS), BF16),
            pltpu.VMEM((C, ROWS, COLS), BF16),
            pltpu.SemaphoreType.DMA((2 * PIECES + 1,)),
        ],
    )(scales, members, observed)
    recv = lax.all_to_all(pay, ("y", "xl", "core"), 0, 0, tiled=True)
    up, down = from_ahead(members[0], 2), from_ahead(members[0], -2)
    msg, zall, token = call(
        distance_kernel,
        (shape((128, 1, 128), F32), shape((M, 8, 128), F32), shape((8, 128), F32)),
        [VMEM, VMEM],
        LONG,
        out_specs=(VMEM, VMEM, VMEM),
        scratch_shapes=[pltpu.VMEM((128, 128), F32)],
    )(recv, aux)
    msg = lax.all_to_all(msg, ("y", "xh", "xl", "core"), 0, 0, tiled=True)
    stack, tile = shape((2 * C, ROWS, COLS), BF16), shape((C, ROWS, COLS), BF16)
    ups, downs, again = call(stack_kernel, (stack, stack, tile), [VMEM] * 4, 1 << 22, out_specs=(VMEM,) * 3)(
        members, up, down, token
    )
    ups, downs, again = from_ahead(ups, 1), from_ahead(downs, -1), from_ahead(again, 2)
    msg = call(relay_kernel, shape((8, 1, 128), F32), [VMEM], LONG, out_specs=VMEM)(msg)
    msg = lax.all_to_all(msg, "z", 0, 0, tiled=True)
    coef, begun = call(
        coefficient_kernel,
        (shape((16, 128), F32), shape((C, ROWS, COLS), F32)),
        [VMEM] * 6,
        1 << 16,
        out_specs=(VMEM, VMEM),
        scratch_shapes=[pltpu.VMEM((CELLS, 128), F32)],
    )(msg, zall, observed, members, down, up)
    return call(
        mix_kernel,
        shape((1, C, ROWS, COLS), F32),
        [VMEM] * 7,
        1 << 22,
        out_specs=hbm,
        scratch_shapes=[pltpu.VMEM((C, ROWS, COLS), F32), pltpu.SemaphoreType.DMA((PARTS,))],
    )(aux, coef, begun, members, ups, downs, again)


def solution(mesh):
    fine = Mesh(mesh.devices.reshape(8, 8, 4, 2, 2), ("y", "z", "xh", "xl", "core"))
    placed = P("y", None, ("z", "xh"), ("xl", "core"))
    return jax.shard_map(
        per_device,
        mesh=fine,
        in_specs=(placed, P(None, ("z", "xh"), ("xl", "core")), P()),
        out_specs=placed,
        check_vma=False,
    )
```

```python
import functools

import jax
import jax.numpy as jnp
import numpy as np
from jax import lax
from jax.experimental import pallas as pl
from jax.experimental.pallas import tpu as pltpu
from jax.sharding import Mesh
from jax.sharding import PartitionSpec as P

BAND = 1.0
F32 = jnp.float32
BF16 = jnp.bfloat16
C, M, LAT, LON = 16, 8, 768, 1024
ROWS, COLS = 24, 256
CELLS = C * ROWS
FIRST = 8
INV = 16
PIECES = 4
PARTS = 16
GROUP = 32
LONG = 1 << 36
HIGHEST = lax.Precision.HIGHEST


def total_weight():
    index = np.arange(LAT).astype(np.float32)
    angle = (np.float32(-90.0) + (index + np.float32(0.5)) * np.float32(180.0) / np.float32(LAT)) * np.float32(
        np.pi / 180.0
    )
    return float(np.sum(np.cos(angle.astype(np.float32)).astype(np.float64)))


SUMW = total_weight()


def row_weight(index):
    angle = (-90.0 + (index.astype(F32) + 0.5) * 180.0 / LAT) * np.float32(np.pi / 180.0)
    return jnp.cos(angle)


def iota(shape, axis):
    return lax.broadcasted_iota(jnp.int32, shape, axis)


def lat_index():
    return lax.axis_index("z") * 4 + lax.axis_index("xh")


def tile_weights(shape):
    return row_weight(lat_index() * ROWS + iota(shape, 0))


def inverse_square(scales_ref, c, rows=8):
    s = jnp.full((8, 128), scales_ref[c], F32)
    return jnp.concatenate([1.0 / (s * s)] * (rows // 8), axis=0)


def lanes_sum(x):
    ones = jnp.ones((8, COLS), BF16)
    flat = x.reshape(CELLS, COLS).astype(BF16)
    return lax.dot_general(ones, flat, (((1,), (1,)), ((), ())), preferred_element_type=F32)


def pack_kernel(scales_hbm, own_hbm, obs_hbm, pay_ref, aux_ref, scales_ref, own_ref, obs_ref, sems):
    per = C // PIECES
    get_scales = pltpu.make_async_copy(scales_hbm, scales_ref, sems.at[2 * PIECES])
    get_scales.start()
    copies = []
    for i in range(PIECES):
        part = pl.ds(i * per, per)
        copies.append(
            (
                pltpu.make_async_copy(own_hbm.at[0, part], own_ref.at[part], sems.at[2 * i]),
                pltpu.make_async_copy(obs_hbm.at[part], obs_ref.at[part], sems.at[2 * i + 1]),
            )
        )
        for copy in copies[-1]:
            copy.start()

    w = tile_weights((ROWS, 128))
    flat = iota((8, 128), 0) * 128 + iota((8, 128), 1)
    channel = lax.shift_right_logical(flat * 2731, 16)
    weight = row_weight(lat_index() * ROWS + flat - channel * ROWS)
    inv = jnp.zeros((8, 128), F32)
    get_scales.wait()
    for c in range(C):
        one = inverse_square(scales_ref, c)
        aux_ref[INV + c : INV + c + 1] = one[0:1]
        inv = jnp.where(channel == c, one, inv)
    aux_ref[8:16] = weight * inv * np.float32(1.0 / (C * SUMW * GROUP))

    total = jnp.zeros((ROWS, 128), F32)
    for i in range(PIECES):
        for copy in copies[i]:
            copy.wait()
        for c in range(i * per, (i + 1) * per):
            x = own_ref[c].astype(F32)
            d = x - obs_ref[c].astype(F32)
            d = d * d
            total = total + (d[:, :128] + d[:, 128:]) * inverse_square(scales_ref, c, ROWS)
            for h in range(2):
                pay_ref[2 * c + h, 0:16] = x[0:16, h * 128 : (h + 1) * 128].astype(BF16)
    total = total * w
    aux_ref[0:8] = (total[0:8] + total[8:16] + total[16:24]) * np.float32(1.0 / (C * LON * SUMW))

    x = own_ref[...].astype(F32)
    above = lanes_sum(x) - lanes_sum(obs_ref[...].astype(F32))
    row = iota((8, 128), 0)
    extra = jnp.zeros((8, 128), F32)
    for k in range(3):
        z = above[:, k * 128 : (k + 1) * 128]
        high = z.astype(BF16).astype(F32)
        extra = jnp.where(row == k, high, jnp.where(row == k + 3, z - high, extra))
    for d in range(GROUP):
        h = d % 2
        last = jnp.concatenate([x[d // 2, 16:24, h * 128 : (h + 1) * 128], extra], axis=0)
        pay_ref[d, 16:32] = last.astype(BF16)


def distance_kernel(recv_ref, aux_ref, msg_ref, zall_ref, token_ref, rows_ref):
    token_ref[...] = jnp.zeros((8, 128), F32)
    me = lax.axis_index("y")
    inv = aux_ref[pl.ds(INV + me * 2 + lax.axis_index("xl"), 1)]
    w = tile_weights((ROWS, 128)) * (inv * np.float32(1.0 / (C * LON * SUMW)))
    row = iota((8, 128), 0)
    got = [recv_ref[s].astype(F32) for s in range(GROUP)]
    rows_ref[...] = jnp.zeros((128, 128), F32)
    pairs = [(k, m, (m - k) % M) for k in (1, 2, 3, 4) for m in range(M) if k < 4 or m < 4]

    def put(at, value):
        rows_ref[at : at + 1] = jnp.sum(value, axis=0, keepdims=True)

    totals = [jnp.zeros((8, 128), F32) for _ in pairs]
    for t in range(3):
        rows8 = slice(t * 8, t * 8 + 8)
        for p, (_, m, n) in enumerate(pairs):
            acc = None
            for l in range(4):
                d = got[m * 4 + l][rows8] - got[n * 4 + l][rows8]
                acc = d * d if acc is None else acc + d * d
            totals[p] = totals[p] + acc * w[rows8]
    for p, (k, m, _) in enumerate(pairs):
        put((k - 1) * 8 + m, totals[p])
    rows_ref[32:40] = jnp.where(row == me, jnp.sum(aux_ref[0:8], axis=0, keepdims=True), 0.0)

    zw = aux_ref[8:16]
    real = row < 3
    zonal = []
    for m in range(M):
        s = sum(got[m * 4 + l][24:32] for l in range(4))
        z = jnp.where(real, s + jnp.concatenate([s[3:8], s[0:3]], axis=0), 0.0) * np.float32(1.0 / LON)
        zonal.append(z)
        zall_ref[m] = z
    for k, m, n in pairs:
        d = zonal[m] - zonal[n]
        put(40 + (k - 1) * 8 + m, zw * d * d)
    for m in range(M):
        put(72 + m, zw * zonal[m] * zonal[m])
    ones = jnp.ones((8, 128), F32)
    sums = lax.dot_general(
        ones, rows_ref[...], (((1,), (1,)), ((), ())), precision=HIGHEST, preferred_element_type=F32
    )
    msg_ref[...] = jnp.broadcast_to(sums[0:1][None], msg_ref.shape)


def relay_kernel(in_ref, out_ref):
    total = jnp.sum(in_ref[...], axis=0)
    out_ref[...] = jnp.broadcast_to(total[None], out_ref.shape)


def stack_kernel(own_ref, up_ref, down_ref, token_ref, ups_ref, downs_ref):
    ups_ref[0:C] = up_ref[...]
    ups_ref[C : 2 * C] = down_ref[...]
    ups_ref[2 * C :] = own_ref[0, 0:FIRST]
    downs_ref[0:C] = own_ref[0]
    downs_ref[C : 2 * C] = down_ref[...]
    downs_ref[2 * C :] = up_ref[FIRST:]


def coefficient_kernel(msg_ref, zall_ref, obs_ref, own_ref, down_ref, up_ref, coef_ref, begun_ref, zcol_ref):
    me = lax.axis_index("y")
    dist = jnp.sum(msg_ref[...], axis=0)
    row, lane = iota((16, 128), 0), iota((16, 128), 1)
    j = row & 7
    k = j + 1
    at = jnp.where(
        k <= 3,
        j * 8 + ((me + k) & 7),
        jnp.where(k == 4, 24 + (me & 3), jnp.where(k <= 7, (7 - k) * 8 + me, 32 + me)),
    )
    at = at + jnp.where(row >= 8, 40, 0)
    e = jnp.broadcast_to(jnp.exp(dist * np.float32(-0.5 / BAND)), (16, 128))
    picked = jnp.sum(jnp.where(lane == at, e, 0.0), axis=1, keepdims=True)
    norm = jnp.where(j == 7, 1.0 / (M * BAND), 1.0 / (M * (M - 1) * BAND))
    coef = jnp.broadcast_to(picked, (16, 128)) * norm
    coef_ref[...] = coef
    zme = zall_ref[me]
    z = coef[15:16] * zme
    for k in range(1, M):
        z = z + coef[7 + k : 8 + k] * (zall_ref[(me + k) & 7] - zme)
    for b in range(3):
        zcol_ref[b * 128 : (b + 1) * 128] = jnp.broadcast_to(z[b : b + 1], (128, 128)).T
    coef = jnp.concatenate([coef, coef], axis=1)
    for c in range(C):
        xm = own_ref[0, c].astype(F32)
        acc = coef[7:8] * (xm - obs_ref[c].astype(F32))
        acc = acc + coef[1:2] * (up_ref[c].astype(F32) - xm)
        acc = acc + coef[4:5] * (down_ref[c].astype(F32) - xm)
        z = zcol_ref[c * ROWS : (c + 1) * ROWS]
        begun_ref[c] = acc + jnp.concatenate([z, z], axis=1)


def mix_kernel(aux_ref, coef_ref, begun_ref, own_ref, ups_ref, downs_ref, out_hbm, out_ref, sems):
    def tile(k, c):
        if k == 1:
            return ups_ref[2 * C + c] if c < FIRST else downs_ref[2 * C + c - FIRST]
        return {3: ups_ref, 6: ups_ref, 7: downs_ref, 4: downs_ref}[k][c + (C if k in (6, 4) else 0)]

    fac = tile_weights((ROWS, 128)) * np.float32(LAT / SUMW)
    coef = coef_ref[...]
    coef = jnp.concatenate([coef, coef], axis=1)
    per = C // PARTS
    copies = []
    for c in range(C):
        xm = own_ref[0, c].astype(F32)
        acc = begun_ref[c]
        for k in (1, 3, 4, 6, 7):
            acc = acc + coef[k - 1 : k] * (tile(k, c).astype(F32) - xm)
        f = fac * aux_ref[INV + c : INV + c + 1]
        out_ref[c] = acc * jnp.concatenate([f, f], axis=1)
        if c % per == per - 1:
            part = pl.ds(c + 1 - per, per)
            copies.append(pltpu.make_async_copy(out_ref.at[part], out_hbm.at[0, part], sems.at[c // per]))
            copies[-1].start()
    for copy in copies:
        copy.wait()


VMEM = pl.BlockSpec(memory_space=pltpu.VMEM)
SMEM = pl.BlockSpec(memory_space=pltpu.SMEM)


def call(kernel, out_shape, in_specs, cost, vmem=32, **kw):
    return pl.pallas_call(
        kernel,
        out_shape=out_shape,
        in_specs=in_specs,
        cost_estimate=pl.CostEstimate(flops=cost, bytes_accessed=cost, transcendentals=0),
        compiler_params=pltpu.CompilerParams(vmem_limit_bytes=vmem * 1024 * 1024),
        **kw,
    )


def from_ahead(tile, k):
    return lax.ppermute(tile, "y", [((i + k) % M, i) for i in range(M)])


def per_device(members, observed, scales):
    shape = jax.ShapeDtypeStruct
    hbm = pl.BlockSpec(memory_space=pltpu.HBM)
    pay, aux = call(
        pack_kernel,
        (shape((GROUP, 32, 128), BF16), shape((INV + C, 128), F32)),
        [hbm] * 3,
        1 << 20,
        vmem=60,
        out_specs=(VMEM, VMEM),
        scratch_shapes=[
            pltpu.SMEM((C,), F32),
            pltpu.VMEM((C, ROWS, COLS), BF16),
            pltpu.VMEM((C, ROWS, COLS), BF16),
            pltpu.SemaphoreType.DMA((2 * PIECES + 1,)),
        ],
    )(scales, members, observed)
    recv = lax.all_to_all(pay, ("y", "xl", "core"), 0, 0, tiled=True)
    up, down = from_ahead(members[0], 2), from_ahead(members[0], -3)
    msg, zall, token = call(
        distance_kernel,
        (shape((128, 1, 128), F32), shape((M, 8, 128), F32), shape((8, 128), F32)),
        [VMEM, VMEM],
        LONG,
        out_specs=(VMEM, VMEM, VMEM),
        scratch_shapes=[pltpu.VMEM((128, 128), F32)],
    )(recv, aux)
    msg = lax.all_to_all(msg, ("y", "xh", "xl", "core"), 0, 0, tiled=True)
    stacks = tuple(shape((2 * C + n, ROWS, COLS), BF16) for n in (FIRST, C - FIRST))
    ups, downs = call(stack_kernel, stacks, [VMEM] * 4, 1 << 22, out_specs=(VMEM,) * 2)(
        members, up, down, token
    )
    ups, downs = from_ahead(ups, 1), from_ahead(downs, -1)
    msg = call(relay_kernel, shape((8, 1, 128), F32), [VMEM], LONG, out_specs=VMEM)(msg)
    msg = lax.all_to_all(msg, "z", 0, 0, tiled=True)
    coef, begun = call(
        coefficient_kernel,
        (shape((16, 128), F32), shape((C, ROWS, COLS), F32)),
        [VMEM] * 6,
        1 << 16,
        out_specs=(VMEM, VMEM),
        scratch_shapes=[pltpu.VMEM((CELLS, 128), F32)],
    )(msg, zall, observed, members, down, up)
    return call(
        mix_kernel,
        shape((1, C, ROWS, COLS), F32),
        [VMEM] * 6,
        1 << 22,
        out_specs=hbm,
        scratch_shapes=[pltpu.VMEM((C, ROWS, COLS), F32), pltpu.SemaphoreType.DMA((PARTS,))],
    )(aux, coef, begun, members, ups, downs)


def solution(mesh):
    fine = Mesh(mesh.devices.reshape(8, 8, 4, 2, 2), ("y", "z", "xh", "xl", "core"))
    placed = P("y", None, ("z", "xh"), ("xl", "core"))
    return jax.shard_map(
        per_device,
        mesh=fine,
        in_specs=(placed, P(None, ("z", "xh"), ("xl", "core")), P()),
        out_specs=placed,
        check_vma=False,
    )
```
